32 devices in a mesh: grp: 4 (over x, core), dev: 8 (over z, y).
Axes of the slice: x: 2, y: 2, z: 4, core: 2. Of those that a mesh axis runs over, the one named last changes fastest.
Arguments:
- wavefield: float32 [32, 2, 128, 2048], P(('grp', 'dev')), may hold values from -6 to 6
- measured: float32 [32, 128, 2048], P(('grp', 'dev')), may hold values from 0.5 to 4
- leaf_map: float32 [32, 2, 128, 128], P(('grp', 'dev')), may hold values from -0.375 to 0.375
- factors: float32 [8, 32, 2, 128, 128], P(None, ('grp', 'dev')), may hold values from -0.375 to 0.375
- closing: float32 [32, 2, 128, 128], P(('grp', 'dev')), may hold values from -0.375 to 0.375
- box_perm: int32 [32, 2048], P(('grp', 'dev')), may hold values from 0 to 2047, each once within a row
- factor_order: int32 [8], replicated, may hold values from 0 to 7, each once
Outputs:
- projected: float32 [32, 2, 128, 2048], P(('grp', 'dev'))
The draws below stay inside these ranges and needn't reach their ends.
Inputs may be any that keep to these rules, and one draw needn't show every extreme that they name: `box_perm`: each row is a permutation of 0 .. 2047. `factor_order`: a permutation of 0 .. 7.
All inputs are finite; a program needn't handle non-finite values.
Results may differ from the reference program's by a relative error of at most 0.00018.
Values sent between devices are 32-bit elements; how exact they have to be, the bound alone decides.
No kernel may reach another device: no remote copies, remote signals or barrier semaphores. Data moves between devices by JAX's collectives and lax.ppermute only.
A program may use at most 64 MiB of HBM per device.

```python
import math
import jax
import jax.numpy as jnp
from jax import lax

R = 64
K = 128
M = 128
Q = 2048
LEVELS = 8
SLABS = 32
N_DEV = 8


def level_of(rng, extent, shards, low, high):
    gain, own = 1.0, jax.random.fold_in(rng, 6)
    for dim, shards_of in shards:
        heights = jnp.exp(jax.random.uniform(jax.random.fold_in(own, dim), (shards_of,), jnp.float32, low / len(shards), high / len(shards)))
        gain = gain * jnp.repeat(heights, extent[dim] // shards_of).reshape([-1 if axis == dim else 1 for axis in range(len(extent))])
    return gain


def centred(key, shape, spread, limit, cuts=(), kind=jnp.bfloat16):
    loudness = level_of(key, shape, cuts, -0.22, 0.18) if cuts else 1.0
    drawn = jax.random.normal(key, shape, jnp.float32) * spread * loudness
    return jnp.minimum(jnp.maximum(drawn, -limit), limit).astype(kind)


def setup_inputs(seed: int = 0) -> dict:
    splits = jax.random.split(jax.random.key(seed), 8)
    return {
        "wavefield": centred(splits[0], (SLABS, 2, M, Q), 1.0, 6.0, ((0, 32),), jnp.float32),
        "measured": jnp.clip(jnp.exp(math.log(4.0) - 2.0794415 * jax.random.uniform(splits[1], (SLABS, M, Q), jnp.float32) ** level_of(splits[1], (SLABS, M, Q), ((0, 32),), -0.2, 0.2)), 0.5, 4.0),
        "leaf_map": centred(splits[2], (SLABS, 2, K, M), (2 * M) ** -0.5, 0.375, ((0, 32),), jnp.float32),
        "factors": centred(splits[3], (LEVELS, SLABS, 2, K, K), (2 * K) ** -0.5, 0.375, ((1, 32),), jnp.float32),
        "closing": centred(splits[4], (SLABS, 2, M, K), (2 * K) ** -0.5, 0.375, ((0, 32),), jnp.float32),
        "box_perm": jax.vmap(lambda own: jax.random.permutation(own, Q))(jax.random.split(splits[5], SLABS)).reshape((SLABS, Q)).astype(jnp.int32),
        "factor_order": jax.random.permutation(splits[6], LEVELS).astype(jnp.int32),
    }


def complex_product(matrix, vectors):
    highest = lax.Precision.HIGHEST
    real_part = jnp.einsum('pxy,pyz->pxz', matrix[:, 0], vectors[:, 0], precision=highest) - jnp.einsum('pxy,pyz->pxz', matrix[:, 1], vectors[:, 1], precision=highest)
    imag_part = jnp.einsum('pxy,pyz->pxz', matrix[:, 0], vectors[:, 1], precision=highest) + jnp.einsum('pxy,pyz->pxz', matrix[:, 1], vectors[:, 0], precision=highest)
    return jnp.stack([real_part, imag_part], axis=1)

def level_bit(level_at):
    dev_bits = N_DEV.bit_length() - 1
    if level_at < 2:
        return dev_bits + 1 - level_at
    return (level_at - 2) % dev_bits

def reference(wavefield, measured, leaf_map, factors, closing, box_perm, factor_order):
    coeffs = complex_product(leaf_map, wavefield)
    for level_at in range(LEVELS):
        bit_at = level_bit(level_at)
        shaped = coeffs.reshape(SLABS >> bit_at + 1, 2, 1 << bit_at, 2, 2, R, Q)
        coeffs = jnp.swapaxes(shaped, 1, 4).reshape(SLABS, 2, K, Q)
        coeffs = complex_product(factors[factor_order[level_at]], coeffs)
        if level_at == LEVELS // 2 - 1:
            coeffs = jnp.take_along_axis(coeffs, box_perm[:, None, None, :], axis=3)
    image = complex_product(closing, coeffs)
    modulus = jnp.sqrt(jnp.maximum(image[:, 0] * image[:, 0] + image[:, 1] * image[:, 1], 0.25))
    return measured[:, None] * image / modulus[:, None]
```

```python
import functools

import jax
import jax.numpy as jnp
from jax import lax
from jax.experimental import pallas as pl
from jax.experimental.pallas import tpu as pltpu
from jax.sharding import PartitionSpec as P

BF = jnp.bfloat16
F32 = jnp.float32
FIRST_SIXTEENTHS = (1, 3, 4, 4, 4)
SECOND_SIXTEENTHS = (2, 4, 5, 5)
TILE = 256


def levels_of(level_count, dev_size):
    dev_bits = dev_size.bit_length() - 1
    return [
        ("grp", 1 - j) if j < 2 else ("dev", (j - 2) % dev_bits)
        for j in range(level_count)
    ]


def swapped(block, level):
    axis, bit = level
    count = lax.axis_size(axis)
    return lax.ppermute(block, axis, [(i, i ^ 1 << bit) for i in range(count)])


def half_bit(level):
    return lax.axis_index(level[0]) >> level[1] & 1


def cuts(sixteenths, boxes):
    unit = boxes // 16
    parts, at = [], 0
    for share in sixteenths:
        parts.append((at, share * unit))
        at += share * unit
    return parts


def split(values):
    high = values.astype(BF)
    return high, (values - high.astype(F32)).astype(BF)


def weights(re, im, column_bit, row_bit):
    def ordered(part):
        half = part.shape[0] // 2
        if column_bit is not None:
            turned = jnp.concatenate([part[:, half:], part[:, :half]], axis=1)
            part = jnp.where(column_bit == 1, turned, part)
        if row_bit is not None:
            turned = jnp.concatenate([part[half:], part[:half]], axis=0)
            part = jnp.where(row_bit == 1, turned, part)
        return part

    re, im = ordered(re), ordered(im)
    return split(
        jnp.concatenate(
            [jnp.concatenate([re, -im], axis=1), jnp.concatenate([im, re], axis=1)],
            axis=0,
        )
    )


def dot(a, b):
    return jnp.dot(a, b, preferred_element_type=F32)


def product(w, z):
    return dot(w[0], z[0]) + (dot(w[0], z[1]) + dot(w[1], z[0]))


def tiles(width):
    step = min(TILE, width)
    return [slice(at, min(at + step, width)) for at in range(0, width, step)]


def put_halves(result, keep_ref, send_ref, cols):
    half = result.shape[0] // 4
    for part in range(2):
        keep_ref[part, :, cols] = result[2 * part * half : (2 * part + 1) * half]
        send_ref[part, :, cols] = result[(2 * part + 1) * half : (2 * part + 2) * half]


def stacked(keep, recv):
    return jnp.concatenate([keep[0], recv[0], keep[1], recv[1]], axis=0)


def leaf_kernel(level, field_ref, leaf_ref, keep_ref, send_ref):
    w = weights(leaf_ref[0, 0], leaf_ref[0, 1], None, half_bit(level))
    for cols in tiles(keep_ref.shape[2]):
        field = field_ref[0, :, :, cols]
        z = split(field.reshape(-1, field.shape[-1]))
        put_halves(product(w, z), keep_ref, send_ref, cols)


def level_kernel(level, following, order_ref, factor_ref, keep_in, recv_in, keep_ref, send_ref):
    w = weights(factor_ref[0, 0, 0], factor_ref[0, 0, 1], half_bit(level), half_bit(following))
    for cols in tiles(keep_ref.shape[2]):
        z = split(stacked(keep_in[:, :, cols], recv_in[:, :, cols]))
        put_halves(product(w, z), keep_ref, send_ref, cols)


def picked(perm, terms, width):
    total = None
    for rows in tiles(terms.shape[1]):
        depth = rows.stop - rows.start
        at = lax.broadcasted_iota(jnp.int32, (depth, width), 0) + rows.start
        chosen = jnp.where(at == perm, 1.0, 0.0).astype(BF)
        here = dot(terms[:, rows], chosen)
        total = here if total is None else total + here
    return total.astype(BF)


def switch_kernel(level, following, order_ref, factor_ref, own_perm, other_perm, keep_in, recv_in, keep_ref, send_ref):
    w = weights(factor_ref[0, 0, 0], factor_ref[0, 0, 1], half_bit(level), half_bit(following))
    half = keep_ref.shape[1]
    for cols in tiles(keep_ref.shape[2]):
        width = cols.stop - cols.start
        keep = picked(own_perm[:, cols], keep_in, width)
        recv = picked(other_perm[:, cols], recv_in, width)
        z = [
            stacked(
                [keep[at : at + half], keep[at + half : at + 2 * half]],
                [recv[at : at + half], recv[at + half : at + 2 * half]],
            )
            for at in (0, 2 * half)
        ]
        put_halves(product(w, z), keep_ref, send_ref, cols)


def terms_kernel(parts, *refs):
    out_ref = refs[-1]
    half = out_ref.shape[0] // 4
    for (at, width), ref in zip(parts, refs[:-1]):
        for part in range(2):
            high, low = split(ref[part])
            out_ref[part * half : (part + 1) * half, at : at + width] = high
            out_ref[(2 + part) * half : (3 + part) * half, at : at + width] = low


def last_kernel(level, order_ref, factor_ref, closing_ref, measured_ref, keep_in, recv_in, *rest):
    out_ref = rest[-1]
    w = weights(factor_ref[0, 0, 0], factor_ref[0, 0, 1], half_bit(level), None)
    c = weights(closing_ref[0, 0], closing_ref[0, 1], None, None)
    for cols in tiles(out_ref.shape[3]):
        z = split(stacked(keep_in[:, :, cols], recv_in[:, :, cols]))
        image = product(c, split(product(w, z)))
        half = image.shape[0] // 2
        re, im = image[:half], image[half:]
        scale = measured_ref[0, :, cols] * lax.rsqrt(jnp.maximum(re * re + im * im, 0.25))
        out_ref[0, 0, :, cols] = re * scale
        out_ref[0, 1, :, cols] = im * scale


def whole():
    return pl.BlockSpec(memory_space=pltpu.VMEM)


def elements(*sizes):
    return tuple(pl.Element(size) for size in sizes)


def params():
    return pltpu.CompilerParams(vmem_limit_bytes=32 << 20)


def cost(flops, moved):
    return pl.CostEstimate(flops=int(flops), bytes_accessed=int(moved), transcendentals=0)


def per_device(wavefield, measured, leaf_map, factors, closing, box_perm, factor_order):
    _, _, cells, boxes = wavefield.shape
    level_count, slots = factors.shape[0], factors.shape[3]
    half = slots // 2
    levels = levels_of(level_count, lax.axis_size("dev"))
    switch_at = level_count // 2
    first, second = cuts(FIRST_SIXTEENTHS, boxes), cuts(SECOND_SIXTEENTHS, boxes)
    unit = boxes // 16

    def halves(width):
        return [jax.ShapeDtypeStruct((2, half, width), F32)] * 2

    def product_cost(width, times=1):
        return cost(times * 24 * slots * slots * width, 16 * slots * width)

    def factor_spec(j):
        return pl.BlockSpec((1, 1, 2, slots, slots), lambda i, order: (order[j], 0, 0, 0, 0))

    def spec(ins, outs):
        return pltpu.PrefetchScalarGridSpec(
            num_scalar_prefetch=1, grid=(1,), in_specs=ins, out_specs=outs
        )

    def leaf(part):
        at, width = part
        return pl.pallas_call(
            functools.partial(leaf_kernel, levels[0]),
            grid=(1,),
            out_shape=halves(width),
            in_specs=[
                pl.BlockSpec(elements(1, 2, cells, width), lambda i: (0, 0, 0, at)),
                pl.BlockSpec((1, 2, slots, cells), lambda i: (0, 0, 0, 0)),
            ],
            out_specs=[whole()] * 2,
            compiler_params=params(),
            cost_estimate=product_cost(width),
        )(wavefield, leaf_map)

    def level(j, keep, recv):
        width = keep.shape[2]
        return pl.pallas_call(
            functools.partial(level_kernel, levels[j], levels[j + 1]),
            grid_spec=spec([factor_spec(j), whole(), whole()], [whole()] * 2),
            out_shape=halves(width),
            compiler_params=params(),
            cost_estimate=product_cost(width),
        )(factor_order, factors, keep, recv)

    def terms(blocks):
        return pl.pallas_call(
            functools.partial(terms_kernel, first),
            out_shape=jax.ShapeDtypeStruct((4 * half, boxes), BF),
            in_specs=[whole()] * len(blocks),
            out_specs=whole(),
            compiler_params=params(),
            cost_estimate=cost(0, 12 * slots * boxes),
        )(*blocks)

    def switch(j, part, other_perm, keep, recv):
        at, width = part

        def perm_spec():
            return pl.BlockSpec(elements(1, width), lambda i, order: (0, at))

        return pl.pallas_call(
            functools.partial(switch_kernel, levels[j], levels[j + 1]),
            grid_spec=spec(
                [factor_spec(j), perm_spec(), perm_spec(), whole(), whole()], [whole()] * 2
            ),
            out_shape=halves(width),
            compiler_params=params(),
            cost_estimate=cost(16 * half * boxes * width, 32 * half * width),
        )(factor_order, factors, box_perm, other_perm, keep, recv)

    def last(part, keep, recv, so_far):
        at, width = part
        j = level_count - 1
        ins = [
            factor_spec(j),
            pl.BlockSpec((1, 2, cells, slots), lambda i, order: (0, 0, 0, 0)),
            pl.BlockSpec(elements(1, cells, width), lambda i, order: (0, 0, at)),
            whole(),
            whole(),
        ]
        args = [factor_order, factors, closing, measured, keep, recv]
        aliases = {}
        if so_far is not None:
            ins.append(pl.BlockSpec(memory_space=pl.ANY))
            aliases = {len(args): 0}
            args.append(so_far)
        return pl.pallas_call(
            functools.partial(last_kernel, levels[j]),
            grid_spec=spec(
                ins,
                pl.BlockSpec(elements(1, 2, cells, width), lambda i, order: (0, 0, 0, at)),
            ),
            out_shape=jax.ShapeDtypeStruct((1, 2, cells, boxes), F32),
            input_output_aliases=aliases,
            compiler_params=params(),
            cost_estimate=product_cost(width, 2),
        )(*args)

    other_perm = swapped(box_perm, levels[switch_at])
    kept, received = [], []
    for part in first:
        keep, send = leaf(part)
        for j in range(switch_at):
            keep, send = level(j, keep, swapped(send, levels[j]))
        kept.append(keep)
        received.append(swapped(send, levels[switch_at]))
    keep_terms, recv_terms = terms(kept), terms(received)
    out = None
    for part in second:
        keep, send = switch(switch_at, part, other_perm, keep_terms, recv_terms)
        for j in range(switch_at + 1, level_count - 1):
            keep, send = level(j, keep, swapped(send, levels[j]))
        out = last(part, keep, swapped(send, levels[level_count - 1]), out)
    return out


def solution(mesh):
    return jax.shard_map(
        per_device,
        mesh=mesh,
        in_specs=(
            P(("grp", "dev"), None, None, None),
            P(("grp", "dev"), None, None),
            P(("grp", "dev"), None, None, None),
            P(None, ("grp", "dev"), None, None, None),
            P(("grp", "dev"), None, None, None),
            P(("grp", "dev"), None),
            P(),
        ),
        out_specs=P(("grp", "dev"), None, None, None),
        check_vma=False,
    )
```

```python
import functools

import jax
import jax.numpy as jnp
from jax import lax
from jax.experimental import pallas as pl
from jax.experimental.pallas import tpu as pltpu
from jax.sharding import PartitionSpec as P

BF = jnp.bfloat16
F32 = jnp.float32
FIRST_SIXTEENTHS = (2, 3, 4, 4, 3)
SECOND_SIXTEENTHS = (2, 3, 4, 4, 3)
FIRST_STARTS = (0, 0, 1, 3, 6)
SECOND_STARTS = (0, 0, 1, 3, 5)
TILE = 256


def levels_of(level_count, dev_size):
    dev_bits = dev_size.bit_length() - 1
    return [
        ("grp", 1 - j) if j < 2 else ("dev", (j - 2) % dev_bits)
        for j in range(level_count)
    ]


def swapped(block, level, name):
    axis, bit = level
    count = lax.axis_size(axis)
    with jax.named_scope(name):
        return lax.ppermute(block, axis, [(i, i ^ 1 << bit) for i in range(count)])


def half_bit(level):
    return lax.axis_index(level[0]) >> level[1] & 1


def cuts(sixteenths, boxes):
    unit = boxes // 16
    parts, at = [], 0
    for share in sixteenths:
        parts.append((at, share * unit))
        at += share * unit
    return parts


def split(values):
    high = values.astype(BF)
    return high, (values - high.astype(F32)).astype(BF)


def weights(re, im, column_bit, row_bit):
    def ordered(part):
        half = part.shape[0] // 2
        if column_bit is not None:
            turned = jnp.concatenate([part[:, half:], part[:, :half]], axis=1)
            part = jnp.where(column_bit == 1, turned, part)
        if row_bit is not None:
            turned = jnp.concatenate([part[half:], part[:half]], axis=0)
            part = jnp.where(row_bit == 1, turned, part)
        return part

    re, im = ordered(re), ordered(im)
    return split(
        jnp.concatenate(
            [jnp.concatenate([re, -im], axis=1), jnp.concatenate([im, re], axis=1)],
            axis=0,
        )
    )


def dot(a, b):
    return jnp.dot(a, b, preferred_element_type=F32)


def product(w, z):
    return dot(w[0], z[0]) + (dot(w[0], z[1]) + dot(w[1], z[0]))


def tiles(width):
    step = min(TILE, width)
    return [slice(at, min(at + step, width)) for at in range(0, width, step)]


def put_halves(result, keep_ref, send_ref, cols):
    half = result.shape[0] // 4
    for part in range(2):
        keep_ref[part, :, cols] = result[2 * part * half : (2 * part + 1) * half]
        send_ref[part, :, cols] = result[(2 * part + 1) * half : (2 * part + 2) * half]


def stacked(keep, recv):
    return jnp.concatenate([keep[0], recv[0], keep[1], recv[1]], axis=0)


def in_turn(starts, steps, begin, go_on):
    pending, used, part = [], 0, 0
    while part < len(starts) or pending:
        if part < len(starts) and (used >= starts[part] or not pending):
            begin(part)
            pending.append((part, 1))
            part += 1
            continue
        at, step = pending.pop(0)
        go_on(at, step)
        used += 1
        if step < steps:
            pending.append((at, step + 1))


def leaf_kernel(level, parts, field_ref, leaf_ref, *refs):
    count = len(parts)
    outs, turn, rest = refs[: 2 * count], refs[2 * count], refs[2 * count + 1 :]
    fields, leaf, arrived = rest[:count], rest[count], rest[count + 1]
    copies = [pltpu.make_async_copy(leaf_ref, leaf, arrived.at[count])]
    for n, (at, width) in enumerate(parts):
        source = field_ref.at[0, :, :, pl.ds(at, width)]
        copies.append(pltpu.make_async_copy(source, fields[n], arrived.at[n]))
    for copy in copies:
        copy.start()
    copies[0].wait()
    w = weights(leaf[0, 0], leaf[0, 1], None, half_bit(level))
    for n in range(count):
        copies[n + 1].wait()
        for cols in tiles(parts[n][1]):
            field = fields[n][:, :, cols]
            z = split(field.reshape(-1, field.shape[-1]))
            put_halves(product(w, z), outs[2 * n], outs[2 * n + 1], cols)


def after_turn(kernel, turn, *refs):
    kernel(*refs)


def weights_kernel(levels, turn, order_ref, factors_ref, closing_ref, perm_ref, *outs):
    perm_out, closing_out, *factor_outs, next_turn = outs
    perm_out[...] = perm_ref[...]
    for j, out in enumerate(factor_outs):
        at = order_ref[j]
        following = half_bit(levels[j + 1]) if j + 1 < len(levels) else None
        high, low = weights(factors_ref[at, 0, 0], factors_ref[at, 0, 1], half_bit(levels[j]), following)
        out[0], out[1] = high, low
    closing_out[0], closing_out[1] = weights(closing_ref[0, 0], closing_ref[0, 1], None, None)


def put_terms(values, out_ref, cols):
    half = values[0].shape[0]
    for part in range(2):
        high, low = split(values[part])
        out_ref[part * half : (part + 1) * half, cols] = high
        out_ref[(2 + part) * half : (3 + part) * half, cols] = low


def level_kernel(before_switch, turn, w, keep_in, recv_in, *refs):
    keep_ref, send_ref, _ = refs[-3:]
    for cols in tiles(send_ref.shape[2]):
        z = split(stacked(keep_in[:, :, cols], recv_in[:, :, cols]))
        result = product(w, z)
        if before_switch:
            half = result.shape[0] // 4
            parts = [result[at * half : (at + 1) * half] for at in range(4)]
            put_terms((parts[0], parts[2]), keep_ref, cols)
            send_ref[0, :, cols], send_ref[1, :, cols] = parts[1], parts[3]
        else:
            put_halves(result, keep_ref, send_ref, cols)


def picked(perm, parts, width):
    total, at = None, 0
    for part in parts:
        for rows in tiles(part.shape[1]):
            depth = rows.stop - rows.start
            box = lax.broadcasted_iota(jnp.int32, (depth, width), 0) + at
            chosen = jnp.where(box == perm, 1.0, 0.0).astype(BF)
            here = dot(part[:, rows], chosen)
            total = here if total is None else total + here
            at += depth
    return total.astype(BF)


def switch_kernel(start, turn, w, own_perm, other_perm, *refs):
    *parts, keep_ref, send_ref, next_turn = refs
    kept, received = parts[: len(parts) // 2], parts[len(parts) // 2 :]
    half = keep_ref.shape[1]
    for cols in tiles(keep_ref.shape[2]):
        width = cols.stop - cols.start
        where = slice(start + cols.start, start + cols.stop)
        keep = picked(own_perm[:, where], kept, width)
        recv = picked(other_perm[:, where], received, width)
        z = [
            stacked(
                [keep[at : at + half], keep[at + half : at + 2 * half]],
                [recv[at : at + half], recv[at + half : at + 2 * half]],
            )
            for at in (0, 2 * half)
        ]
        put_halves(product(w, z), keep_ref, send_ref, cols)


def terms_kernel(turn, part_ref, out_ref, next_turn):
    for cols in tiles(part_ref.shape[2]):
        put_terms(part_ref[:, :, cols], out_ref, cols)


def last_kernel(turn, w, c, measured_ref, keep_in, recv_in, *rest):
    out_ref = rest[-2]
    for cols in tiles(out_ref.shape[3]):
        z = split(stacked(keep_in[:, :, cols], recv_in[:, :, cols]))
        image = product(c, split(product(w, z)))
        half = image.shape[0] // 2
        re, im = image[:half], image[half:]
        scale = measured_ref[0, :, cols] * lax.rsqrt(jnp.maximum(re * re + im * im, 0.25))
        out_ref[0, 0, :, cols] = re * scale
        out_ref[0, 1, :, cols] = im * scale


def elements(*sizes):
    return tuple(pl.Element(size) for size in sizes)


def whole():
    return pl.BlockSpec(memory_space=pltpu.VMEM)


def anywhere():
    return pl.BlockSpec(memory_space=pl.ANY)


COST = pl.CostEstimate(flops=1000000000, bytes_accessed=2500000, transcendentals=0)


def per_device(wavefield, measured, leaf_map, factors, closing, box_perm, factor_order):
    _, _, cells, boxes = wavefield.shape
    level_count, slots = factors.shape[0], factors.shape[3]
    half = slots // 2
    levels = levels_of(level_count, lax.axis_size("dev"))
    switch_at = level_count // 2
    first, second = cuts(FIRST_SIXTEENTHS, boxes), cuts(SECOND_SIXTEENTHS, boxes)
    params = pltpu.CompilerParams(vmem_limit_bytes=32 << 20)
    turn_shape = jax.ShapeDtypeStruct((8, 128), F32)
    turn = factor_order
    name = "product"

    def call(kernel, ins, args, shapes, **more):
        nonlocal turn, name
        *outs, turn = pl.pallas_call(
            kernel,
            in_specs=[anywhere(), *ins],
            out_specs=[*more.pop("outs", [whole()] * len(shapes)), anywhere()],
            out_shape=[*shapes, turn_shape],
            compiler_params=params,
            cost_estimate=COST,
            name=name,
            **more,
        )(turn, *args)
        return outs

    def halves(width):
        return [jax.ShapeDtypeStruct((2, half, width), F32)] * 2

    def leaf(parts, after):
        nonlocal turn
        stay = pl.BlockSpec(memory_space=pltpu.HBM)
        ins, args = [stay] * 2, [wavefield, leaf_map]
        kernel = functools.partial(leaf_kernel, levels[0], parts)
        if after:
            ins, args = [anywhere()] + ins, [turn] + args
            kernel = functools.partial(after_turn, kernel)
        *outs, turn = pl.pallas_call(
            kernel,
            in_specs=ins,
            out_specs=[*[whole()] * (2 * len(parts)), anywhere()],
            out_shape=[shape for part in parts for shape in halves(part[1])] + [turn_shape],
            scratch_shapes=[
                *[pltpu.VMEM((2, cells, part[1]), F32) for part in parts],
                pltpu.VMEM(leaf_map.shape, F32),
                pltpu.SemaphoreType.DMA((len(parts) + 1,)),
            ],
            compiler_params=pltpu.CompilerParams(vmem_limit_bytes=(32 if after else 61) << 20),
            cost_estimate=COST,
            name="leaf",
        )(*args)
        return list(zip(outs[::2], outs[1::2]))

    def prepared():
        matrix = jax.ShapeDtypeStruct((2, 2 * slots, 2 * slots), BF)
        shapes = [jax.ShapeDtypeStruct(box_perm.shape, box_perm.dtype)] + [matrix] * (level_count + 1)
        perm, closing_terms, *factor_terms = call(
            functools.partial(weights_kernel, levels),
            [pl.BlockSpec(memory_space=pltpu.SMEM)] + [whole()] * 3,
            [factor_order, factors, closing, box_perm],
            shapes,
        )
        return perm, closing_terms, factor_terms

    def terms_of(width):
        return jax.ShapeDtypeStruct((4 * half, width), BF)

    def level(w, keep, recv, before_switch=False, also=()):
        width = recv.shape[2]
        shapes = halves(width)
        if before_switch:
            shapes[0] = terms_of(width)
        kernel = functools.partial(level_kernel, before_switch)
        ins = [whole()] * 3 + [anywhere()] * len(also)
        return call(kernel, ins, [w, keep, recv, *also], shapes)

    def terms(block):
        return call(terms_kernel, [whole()], [block], [terms_of(block.shape[2])])[0]

    def switch(part, w, own_perm, other_perm, keep, recv):
        at, width = part
        return call(
            functools.partial(switch_kernel, at),
            [whole()] * (3 + len(keep) + len(recv)), [w, own_perm, other_perm, *keep, *recv],
            halves(width),
        )

    def last(part, w, c, keep, recv, so_far):
        at, width = part
        ins = [whole()] * 5
        args = [w, c, lax.slice_in_dim(measured, at, at + width, axis=2), keep, recv]
        aliases = {}
        if so_far is not None:
            ins.append(anywhere())
            aliases = {len(args) + 1: 0}
            args.append(so_far)
        return call(
            last_kernel, ins, args,
            [jax.ShapeDtypeStruct((1, 2, cells, boxes), F32)],
            outs=[pl.BlockSpec(elements(1, 2, cells, width), lambda i: (0, 0, 0, at))],
            grid=(1,), input_output_aliases=aliases,
        )[0]

    own, away = {}, {}

    def leave(part, step, keep, send):
        own[part], away[part] = keep, swapped(send, levels[step], f"send_{part}_{step}")

    first_leaf = leaf(first[:1], False)
    leaves = first_leaf + leaf(first[1:], True)
    name = "weights"
    own_perm, closing_terms, factor_terms = prepared()
    other_perm = swapped(own_perm, levels[switch_at], "send_order")

    def first_begin(part):
        leave(part, 0, *leaves[part])

    def first_step(part, step):
        nonlocal name
        name = f"part_{part}_{step}"
        if step > switch_at:
            away[part] = terms(away[part])
        else:
            w = factor_terms[step - 1]
            also = [other_perm] if (part, step) == (0, 1) else []
            leave(part, step, *level(w, own[part], away[part], step == switch_at, also))

    in_turn(FIRST_STARTS, switch_at + 1, first_begin, first_step)
    kept, received = ([held[part] for part in range(len(first))] for held in (own, away))
    out = None

    def second_begin(part):
        nonlocal name
        name = f"again_{part}_{switch_at}"
        w = factor_terms[switch_at]
        leave(part, switch_at + 1, *switch(second[part], w, own_perm, other_perm, kept, received))

    def second_step(part, step):
        nonlocal name, out
        step += switch_at
        name = f"again_{part}_{step}"
        w = factor_terms[step]
        if step == level_count - 1:
            out = last(second[part], w, closing_terms, own[part], away[part], out)
        else:
            leave(part, step + 1, *level(w, own[part], away[part]))

    in_turn(SECOND_STARTS, level_count - 1 - switch_at, second_begin, second_step)
    return out


def solution(mesh):
    return jax.shard_map(
        per_device,
        mesh=mesh,
        in_specs=(
            P(("grp", "dev"), None, None, None),
            P(("grp", "dev"), None, None),
            P(("grp", "dev"), None, None, None),
            P(None, ("grp", "dev"), None, None, None),
            P(("grp", "dev"), None, None, None),
            P(("grp", "dev"), None),
            P(),
        ),
        out_specs=P(("grp", "dev"), None, None, None),
        check_vma=False,
    )
```

```python
import functools

import jax
import jax.numpy as jnp
from jax import lax
from jax.experimental import pallas as pl
from jax.experimental.pallas import tpu as pltpu
from jax.sharding import PartitionSpec as P

BF = jnp.bfloat16
F32 = jnp.float32
FIRST_SIXTEENTHS = (3, 3, 4, 4, 2)
SECOND_SIXTEENTHS = (3, 4, 4, 3, 2)
FIRST_STARTS = (0, 0, 1, 3, 6)
SECOND_STARTS = (0, 1, 3, 5, 7)
ORDER_USED = (2, 3)
LATE_ROWS = 32
TILE = 256


def levels_of(level_count, dev_size):
    dev_bits = dev_size.bit_length() - 1
    return [
        ("grp", 1 - j) if j < 2 else ("dev", (j - 2) % dev_bits)
        for j in range(level_count)
    ]


def swapped(block, level, name):
    axis, bit = level
    count = lax.axis_size(axis)
    with jax.named_scope(name):
        return lax.ppermute(block, axis, [(i, i ^ 1 << bit) for i in range(count)])


def half_bit(level):
    return lax.axis_index(level[0]) >> level[1] & 1


def cuts(sixteenths, boxes):
    unit = boxes // 16
    parts, at = [], 0
    for share in sixteenths:
        parts.append((at, share * unit))
        at += share * unit
    return parts


def split(values):
    high = values.astype(BF)
    return high, (values - high.astype(F32)).astype(BF)


def weights(re, im, column_bit, row_bit):
    def ordered(part):
        half = part.shape[0] // 2
        if column_bit is not None:
            turned = jnp.concatenate([part[:, half:], part[:, :half]], axis=1)
            part = jnp.where(column_bit == 1, turned, part)
        if row_bit is not None:
            turned = jnp.concatenate([part[half:], part[:half]], axis=0)
            part = jnp.where(row_bit == 1, turned, part)
        return part

    re, im = ordered(re), ordered(im)
    return split(
        jnp.concatenate(
            [jnp.concatenate([re, -im], axis=1), jnp.concatenate([im, re], axis=1)],
            axis=0,
        )
    )


def dot(a, b):
    return jnp.dot(a, b, preferred_element_type=F32)


def product(w, z):
    return dot(w[0], z[0]) + (dot(w[0], z[1]) + dot(w[1], z[0]))


def tiles(width):
    step = min(TILE, width)
    return [slice(at, min(at + step, width)) for at in range(0, width, step)]


def put_halves(result, keep_ref, send_ref, cols):
    half = result.shape[0] // 4
    for part in range(2):
        keep_ref[part, :, cols] = result[2 * part * half : (2 * part + 1) * half]
        send_ref[part, :, cols] = result[(2 * part + 1) * half : (2 * part + 2) * half]


def stacked(keep, recv):
    return jnp.concatenate([keep[0], recv[0], keep[1], recv[1]], axis=0)


def in_turn(first, second):
    pending, used, begun, ready = [], [0, 0], [0, 0], 0
    phases = (first, second)
    while pending or begun[1] < len(second[0]):
        for phase, (starts, _, begin, _) in enumerate(phases):
            part = begun[phase]
            open_now = phase == 0 or ready == len(first[0])
            if part < len(starts) and open_now and (used[phase] >= starts[part] or not pending):
                begin(part)
                pending.append((phase, part, 1))
                begun[phase] += 1
                break
        else:
            phase, part, step = pending.pop(0)
            _, steps, _, go_on = phases[phase]
            used = [used[0] + 1, used[1] + (ready == len(first[0]))]
            go_on(part, step)
            ready += phase == 0 and step == steps - 1
            if step < steps:
                pending.append((phase, part, step + 1))


def leaf_kernel(level, parts, field_ref, leaf_ref, *refs):
    count = len(parts)
    outs, turn, rest = refs[: 2 * count], refs[2 * count], refs[2 * count + 1 :]
    fields, leaf, arrived = rest[:count], rest[count], rest[count + 1]
    copies = [pltpu.make_async_copy(leaf_ref, leaf, arrived.at[count])]
    for n, (at, width) in enumerate(parts):
        source = field_ref.at[0, :, :, pl.ds(at, width)]
        copies.append(pltpu.make_async_copy(source, fields[n], arrived.at[n]))
    for copy in copies:
        copy.start()
    copies[0].wait()
    w = weights(leaf[0, 0], leaf[0, 1], None, half_bit(level))
    for n in range(count):
        copies[n + 1].wait()
        for cols in tiles(parts[n][1]):
            field = fields[n][:, :, cols]
            z = split(field.reshape(-1, field.shape[-1]))
            put_halves(product(w, z), outs[2 * n], outs[2 * n + 1], cols)


def after_turn(kernel, turn, *refs):
    kernel(*refs)


def weights_kernel(levels, turn, order_ref, factors_ref, closing_ref, perm_ref, *outs):
    perm_out, closing_out, *factor_outs, next_turn = outs
    perm_out[...] = perm_ref[...]
    for j, out in enumerate(factor_outs):
        at = order_ref[j]
        following = half_bit(levels[j + 1]) if j + 1 < len(levels) else None
        high, low = weights(factors_ref[at, 0, 0], factors_ref[at, 0, 1], half_bit(levels[j]), following)
        out[0], out[1] = high, low
    closing_out[0], closing_out[1] = weights(closing_ref[0, 0], closing_ref[0, 1], None, None)


def put_terms(values, out_ref, cols):
    at = 0
    for terms in zip(*(split(value) for value in values)):
        for term in terms:
            out_ref[at : at + term.shape[0], cols] = term
            at += term.shape[0]


def level_kernel(turn, w, keep_in, recv_in, *refs):
    keep_ref, send_ref, _ = refs[-3:]
    for cols in tiles(send_ref.shape[2]):
        z = split(stacked(keep_in[:, :, cols], recv_in[:, :, cols]))
        put_halves(product(w, z), keep_ref, send_ref, cols)


def ready_kernel(turn, w, keep_in, recv_in, *refs):
    own_ref, send_ref, _ = refs[-3:]
    early = send_ref.shape[1]
    for cols in tiles(send_ref.shape[2]):
        z = split(stacked(keep_in[:, :, cols], recv_in[:, :, cols]))
        result = product(w, z)
        slots = result.shape[0] // 2
        half = slots // 2
        own = []
        for part in range(2):
            rows = result[part * slots : (part + 1) * slots]
            own.append(jnp.concatenate([rows[:half], rows[half + early :]], axis=0))
            send_ref[part, :, cols] = rows[half : half + early]
        put_terms(own, own_ref, cols)


def terms_kernel(turn, part_ref, out_ref, next_turn):
    for cols in tiles(part_ref.shape[2]):
        put_terms([part_ref[0, :, cols], part_ref[1, :, cols]], out_ref, cols)


def picked(perm, parts, width):
    total, at = None, 0
    for part in parts:
        for rows in tiles(part.shape[1]):
            depth = rows.stop - rows.start
            box = lax.broadcasted_iota(jnp.int32, (depth, width), 0) + at
            chosen = jnp.where(box == perm, 1.0, 0.0).astype(BF)
            here = dot(part[:, rows], chosen)
            total = here if total is None else total + here
            at += depth
    return total


def pick_own_kernel(start, turn, own_perm, *refs):
    *own, keep_ref, send_ref, _ = refs
    half, late = keep_ref.shape[0] // 4, send_ref.shape[1]
    for cols in tiles(send_ref.shape[2]):
        where = slice(start + cols.start, start + cols.stop)
        rows = picked(own_perm[:, where], own, cols.stop - cols.start)
        at = 0
        for term in range(2):
            for part in range(2):
                to = (2 * term + part) * half
                keep_ref[to : to + half, cols] = rows[at : at + half].astype(BF)
                at += half + late
        high, low = rows[: 2 * (half + late)], rows[2 * (half + late) :]
        for part in range(2):
            at = part * (half + late) + half
            send_ref[part, :, cols] = high[at : at + late] + low[at : at + late]


def switch_kernel(start, turn, w, other_perm, keep_in, late_in, *refs):
    *early, keep_ref, send_ref, _ = refs
    half, late = keep_ref.shape[1], late_in.shape[1]
    rest = half - late
    for cols in tiles(send_ref.shape[2]):
        where = slice(start + cols.start, start + cols.stop)
        recv = picked(other_perm[:, where], early, cols.stop - cols.start).astype(BF)
        late_terms = [split(late_in[part, :, cols]) for part in range(2)]
        z = []
        for term in range(2):
            rows = []
            for part in range(2):
                at = 2 * term + part
                rows.append(keep_in[at * half : (at + 1) * half, cols])
                rows.append(recv[at * rest : (at + 1) * rest])
                rows.append(late_terms[part][term])
            z.append(jnp.concatenate(rows, axis=0))
        put_halves(product(w, z), keep_ref, send_ref, cols)


def last_kernel(turn, w, c, measured_ref, keep_in, recv_in, *rest):
    out_ref = rest[-2]
    for cols in tiles(out_ref.shape[3]):
        z = split(stacked(keep_in[:, :, cols], recv_in[:, :, cols]))
        image = product(c, split(product(w, z)))
        half = image.shape[0] // 2
        re, im = image[:half], image[half:]
        scale = measured_ref[0, :, cols] * lax.rsqrt(jnp.maximum(re * re + im * im, 0.25))
        out_ref[0, 0, :, cols] = re * scale
        out_ref[0, 1, :, cols] = im * scale


def elements(*sizes):
    return tuple(pl.Element(size) for size in sizes)


def whole():
    return pl.BlockSpec(memory_space=pltpu.VMEM)


def anywhere():
    return pl.BlockSpec(memory_space=pl.ANY)


COST = pl.CostEstimate(flops=1000000000, bytes_accessed=2500000, transcendentals=0)


def per_device(wavefield, measured, leaf_map, factors, closing, box_perm, factor_order):
    _, _, cells, boxes = wavefield.shape
    level_count, slots = factors.shape[0], factors.shape[3]
    half = slots // 2
    late = half * LATE_ROWS // 64
    levels = levels_of(level_count, lax.axis_size("dev"))
    switch_at = level_count // 2
    first, second = cuts(FIRST_SIXTEENTHS, boxes), cuts(SECOND_SIXTEENTHS, boxes)
    params = pltpu.CompilerParams(vmem_limit_bytes=32 << 20)
    turn_shape = jax.ShapeDtypeStruct((8, 128), F32)
    turn = factor_order
    name = "product"

    def call(kernel, ins, args, shapes, **more):
        nonlocal turn, name
        *outs, turn = pl.pallas_call(
            kernel,
            in_specs=[anywhere(), *ins],
            out_specs=[*more.pop("outs", [whole()] * len(shapes)), anywhere()],
            out_shape=[*shapes, turn_shape],
            compiler_params=params,
            cost_estimate=COST,
            name=name,
            **more,
        )(turn, *args)
        return outs

    def halves(width):
        return [jax.ShapeDtypeStruct((2, half, width), F32)] * 2

    def leaf(parts, after):
        nonlocal turn
        stay = pl.BlockSpec(memory_space=pltpu.HBM)
        ins, args = [stay] * 2, [wavefield, leaf_map]
        kernel = functools.partial(leaf_kernel, levels[0], parts)
        if after:
            ins, args = [anywhere()] + ins, [turn] + args
            kernel = functools.partial(after_turn, kernel)
        *outs, turn = pl.pallas_call(
            kernel,
            in_specs=ins,
            out_specs=[*[whole()] * (2 * len(parts)), anywhere()],
            out_shape=[shape for part in parts for shape in halves(part[1])] + [turn_shape],
            scratch_shapes=[
                *[pltpu.VMEM((2, cells, part[1]), F32) for part in parts],
                pltpu.VMEM(leaf_map.shape, F32),
                pltpu.SemaphoreType.DMA((len(parts) + 1,)),
            ],
            compiler_params=pltpu.CompilerParams(vmem_limit_bytes=(32 if after else 61) << 20),
            cost_estimate=COST,
            name="leaf",
        )(*args)
        return list(zip(outs[::2], outs[1::2]))

    def prepared():
        matrix = jax.ShapeDtypeStruct((2, 2 * slots, 2 * slots), BF)
        shapes = [jax.ShapeDtypeStruct(box_perm.shape, box_perm.dtype)] + [matrix] * (level_count + 1)
        perm, closing_terms, *factor_terms = call(
            functools.partial(weights_kernel, levels),
            [pl.BlockSpec(memory_space=pltpu.SMEM)] + [whole()] * 3,
            [factor_order, factors, closing, box_perm],
            shapes,
        )
        return perm, closing_terms, factor_terms

    def terms_of(rows, width):
        return jax.ShapeDtypeStruct((4 * rows, width), BF)

    def block_of(rows, width):
        return jax.ShapeDtypeStruct((2, rows, width), F32)

    def level(w, keep, recv, ready=False, also=()):
        width = recv.shape[2]
        shapes = halves(width)
        if ready:
            shapes = [terms_of(half + late, width), block_of(half - late, width)]
        ins = [whole()] * 3 + [anywhere()] * len(also)
        return call(ready_kernel if ready else level_kernel, ins, [w, keep, recv, *also], shapes)

    def terms(block):
        return call(terms_kernel, [whole()], [block], [terms_of(*block.shape[1:])])[0]

    def pick_own(part, own_perm, parts):
        at, width = part
        kernel = functools.partial(pick_own_kernel, at)
        shapes = [terms_of(half, width), block_of(late, width)]
        return call(kernel, [whole()] * (1 + len(parts)), [own_perm, *parts], shapes)

    def switch(part, w, other_perm, keep, late_rows, early):
        at, width = part
        kernel = functools.partial(switch_kernel, at)
        args = [w, other_perm, keep, late_rows, *early]
        return call(kernel, [whole()] * len(args), args, halves(width))

    def last(part, w, c, keep, recv, so_far):
        at, width = part
        ins = [whole()] * 5
        args = [w, c, lax.slice_in_dim(measured, at, at + width, axis=2), keep, recv]
        aliases = {}
        if so_far is not None:
            ins.append(anywhere())
            aliases = {len(args) + 1: 0}
            args.append(so_far)
        return call(
            last_kernel, ins, args,
            [jax.ShapeDtypeStruct((1, 2, cells, boxes), F32)],
            outs=[pl.BlockSpec(elements(1, 2, cells, width), lambda i: (0, 0, 0, at))],
            grid=(1,), input_output_aliases=aliases,
        )[0]

    own, away = {}, {}

    def leave(part, step, keep, send):
        own[part], away[part] = keep, swapped(send, levels[step], f"send_{part}_{step}")

    first_leaf = leaf(first[:1], False)
    leaves = first_leaf + leaf(first[1:], True)
    name = "weights"
    own_perm, closing_terms, factor_terms = prepared()
    other_perm = swapped(own_perm, levels[switch_at], "send_order")

    def first_begin(part):
        leave(part, 0, *leaves[part])

    def first_step(part, step):
        nonlocal name
        name = f"part_{part}_{step}"
        if step > switch_at:
            away[part] = terms(away[part])
        else:
            w = factor_terms[step - 1]
            also = [other_perm] if (part, step) == ORDER_USED else []
            leave(part, step, *level(w, own[part], away[part], step == switch_at, also))

    def second_begin(part):
        nonlocal name
        name = f"again_{part}_{switch_at - 1}"
        kept = [own[n] for n in range(len(first))]
        keep, send = pick_own(second[part], own_perm, kept)
        own2[part], away2[part] = keep, swapped(send, levels[switch_at], f"send_{part}_late")

    def second_step(part, step):
        nonlocal name, out
        step += switch_at - 1
        name = f"again_{part}_{step}"
        w = factor_terms[step]
        if step == level_count - 1:
            out = last(second[part], w, closing_terms, own2[part], away2[part], out)
            return
        if step == switch_at:
            early = [away[n] for n in range(len(first))]
            keep, send = switch(second[part], w, other_perm, own2[part], away2[part], early)
        else:
            keep, send = level(w, own2[part], away2[part])
        own2[part], away2[part] = keep, swapped(send, levels[step + 1], f"send_{part}_{step + 1}")

    own2, away2, out = {}, {}, None
    in_turn(
        (FIRST_STARTS, switch_at + 1, first_begin, first_step),
        (SECOND_STARTS, level_count - switch_at, second_begin, second_step),
    )
    return out


def solution(mesh):
    return jax.shard_map(
        per_device,
        mesh=mesh,
        in_specs=(
            P(("grp", "dev"), None, None, None),
            P(("grp", "dev"), None, None),
            P(("grp", "dev"), None, None, None),
            P(None, ("grp", "dev"), None, None, None),
            P(("grp", "dev"), None, None, None),
            P(("grp", "dev"), None),
            P(),
        ),
        out_specs=P(("grp", "dev"), None, None, None),
        check_vma=False,
    )
```

```python
import functools

import jax
import jax.numpy as jnp
from jax import lax
from jax.experimental import pallas as pl
from jax.experimental.pallas import tpu as pltpu
from jax.sharding import PartitionSpec as P

BF = jnp.bfloat16
F32 = jnp.float32
FIRST_SIXTEENTHS = (3, 3, 4, 4, 2)
SECOND_SIXTEENTHS = (3, 3, 4, 4, 2)
FIRST_STARTS = (0, 0, 1, 3, 6)
SECOND_STARTS = (0, 1, 3, 5, 8)
LATE_ROWS = 32
ORDER_ROWS = 8
TILE = 256


def levels_of(level_count, dev_size):
    dev_bits = dev_size.bit_length() - 1
    return [
        ("grp", 1 - j) if j < 2 else ("dev", (j - 2) % dev_bits)
        for j in range(level_count)
    ]


def swapped(block, level, name):
    axis, bit = level
    count = lax.axis_size(axis)
    with jax.named_scope(name):
        return lax.ppermute(block, axis, [(i, i ^ 1 << bit) for i in range(count)])


def half_bit(level):
    return lax.axis_index(level[0]) >> level[1] & 1


def cuts(sixteenths, boxes):
    unit = boxes // 16
    parts, at = [], 0
    for share in sixteenths:
        parts.append((at, share * unit))
        at += share * unit
    return parts


def split(values):
    high = values.astype(BF)
    return high, (values - high.astype(F32)).astype(BF)


def weights(re, im, column_bit, row_bit):
    def ordered(part):
        half = part.shape[0] // 2
        if column_bit is not None:
            turned = jnp.concatenate([part[:, half:], part[:, :half]], axis=1)
            part = jnp.where(column_bit == 1, turned, part)
        if row_bit is not None:
            turned = jnp.concatenate([part[half:], part[:half]], axis=0)
            part = jnp.where(row_bit == 1, turned, part)
        return part

    re, im = ordered(re), ordered(im)
    return split(
        jnp.concatenate(
            [jnp.concatenate([re, -im], axis=1), jnp.concatenate([im, re], axis=1)],
            axis=0,
        )
    )


def dot(a, b):
    return jnp.dot(a, b, preferred_element_type=F32)


def product(w, z):
    return dot(w[0], z[0]) + (dot(w[0], z[1]) + dot(w[1], z[0]))


def tiles(width):
    step = min(TILE, width)
    return [slice(at, min(at + step, width)) for at in range(0, width, step)]


def put_halves(result, keep_ref, send_ref, cols):
    half = result.shape[0] // 4
    for part in range(2):
        keep_ref[part, :, cols] = result[2 * part * half : (2 * part + 1) * half]
        send_ref[part, :, cols] = result[(2 * part + 1) * half : (2 * part + 2) * half]


def stacked(keep, recv):
    return jnp.concatenate([keep[0], recv[0], keep[1], recv[1]], axis=0)


def in_turn(first, second):
    pending, used, begun, ready = [], [0, 0], [0, 0], 0
    phases = (first, second)
    while pending or begun[1] < len(second[0]):
        for phase, (starts, _, begin, _) in enumerate(phases):
            part = begun[phase]
            open_now = phase == 0 or ready == len(first[0])
            if part < len(starts) and open_now and (used[phase] >= starts[part] or not pending):
                begin(part)
                pending.append((phase, part, 1))
                begun[phase] += 1
                break
        else:
            phase, part, step = pending.pop(0)
            _, steps, _, go_on = phases[phase]
            used = [used[0] + 1, used[1] + (ready == len(first[0]))]
            go_on(part, step)
            ready += phase == 0 and step == steps - 1
            if step < steps:
                pending.append((phase, part, step + 1))


def leaf_kernel(level, parts, field_ref, leaf_ref, *refs):
    count = len(parts)
    outs, turn, rest = refs[: 2 * count], refs[2 * count], refs[2 * count + 1 :]
    fields, leaf, arrived = rest[:count], rest[count], rest[count + 1]
    copies = [pltpu.make_async_copy(leaf_ref, leaf, arrived.at[count])]
    for n, (at, width) in enumerate(parts):
        source = field_ref.at[0, :, :, pl.ds(at, width)]
        copies.append(pltpu.make_async_copy(source, fields[n], arrived.at[n]))
    for copy in copies:
        copy.start()
    copies[0].wait()
    w = weights(leaf[0, 0], leaf[0, 1], None, half_bit(level))
    for n in range(count):
        copies[n + 1].wait()
        for cols in tiles(parts[n][1]):
            field = fields[n][:, :, cols]
            z = split(field.reshape(-1, field.shape[-1]))
            put_halves(product(w, z), outs[2 * n], outs[2 * n + 1], cols)


def after_turn(kernel, turn, *refs):
    kernel(*refs)


def weights_kernel(levels, turn, order_ref, factors_ref, closing_ref, perm_ref, *outs):
    perm_out, closing_out, *factor_outs, next_turn = outs
    perm_out[...] = perm_ref[...]
    for j, out in enumerate(factor_outs):
        at = order_ref[j]
        following = half_bit(levels[j + 1]) if j + 1 < len(levels) else None
        high, low = weights(factors_ref[at, 0, 0], factors_ref[at, 0, 1], half_bit(levels[j]), following)
        out[0], out[1] = high, low
    closing_out[0], closing_out[1] = weights(closing_ref[0, 0], closing_ref[0, 1], None, None)


def put_terms(values, out_ref, cols):
    at = 0
    for terms in zip(*(split(value) for value in values)):
        for term in terms:
            out_ref[at : at + term.shape[0], cols] = term
            at += term.shape[0]


def level_kernel(turn, w, keep_in, recv_in, keep_ref, send_ref, next_turn):
    for cols in tiles(send_ref.shape[2]):
        z = split(stacked(keep_in[:, :, cols], recv_in[:, :, cols]))
        put_halves(product(w, z), keep_ref, send_ref, cols)


def ready_kernel(turn, w, keep_in, recv_in, *refs):
    own_ref, send_ref, _ = refs[-3:]
    early = send_ref.shape[1]
    if len(refs) > 3:
        early -= ORDER_ROWS
        put_order(refs[0], send_ref, early)
    for cols in tiles(send_ref.shape[2]):
        z = split(stacked(keep_in[:, :, cols], recv_in[:, :, cols]))
        result = product(w, z)
        slots = result.shape[0] // 2
        half = slots // 2
        own = []
        for part in range(2):
            rows = result[part * slots : (part + 1) * slots]
            own.append(jnp.concatenate([rows[:half], rows[half + early :]], axis=0))
            send_ref[part, :early, cols] = rows[half : half + early]
        put_terms(own, own_ref, cols)


def order_places(boxes, width):
    places = [(n // ORDER_ROWS, n % ORDER_ROWS, n * width) for n in range(-(-boxes // width))]
    return [(part, row, slice(at, min(at + width, boxes))) for part, row, at in places]


def put_order(perm_ref, send_ref, early):
    boxes, width = perm_ref.shape[1], send_ref.shape[2]
    blank = jnp.zeros((1, width), F32)
    rows = [[blank] * ORDER_ROWS for _ in range(2)]
    for part, row, where in order_places(boxes, width):
        here = perm_ref[:, where].astype(F32)
        if here.shape[1] < width:
            here = jnp.concatenate([here, blank[:, here.shape[1] :]], axis=1)
        rows[part][row] = here
    for part in range(2):
        send_ref[part, early:] = jnp.concatenate(rows[part], axis=0)


def terms_kernel(turn, part_ref, out_ref, *rest):
    early = out_ref.shape[0] // 4
    for cols in tiles(part_ref.shape[2]):
        put_terms([part_ref[part, :early, cols] for part in range(2)], out_ref, cols)
    if len(rest) > 1:
        perm_ref = rest[0]
        for part, row, where in order_places(perm_ref.shape[1], part_ref.shape[2]):
            width = where.stop - where.start
            here = part_ref[part, early + row : early + row + 1, :width]
            perm_ref[:, where] = here.astype(jnp.int32)


def picked(perm, parts, width):
    total, at = None, 0
    for part in parts:
        for rows in tiles(part.shape[1]):
            depth = rows.stop - rows.start
            box = lax.broadcasted_iota(jnp.int32, (depth, width), 0) + at
            chosen = jnp.where(box == perm, 1.0, 0.0).astype(BF)
            here = dot(part[:, rows], chosen)
            total = here if total is None else total + here
            at += depth
    return total


def pick_own_kernel(start, turn, own_perm, *refs):
    *own, keep_ref, send_ref, _ = refs
    half, late = keep_ref.shape[0] // 4, send_ref.shape[1]
    for cols in tiles(send_ref.shape[2]):
        where = slice(start + cols.start, start + cols.stop)
        rows = picked(own_perm[:, where], own, cols.stop - cols.start)
        at = 0
        for term in range(2):
            for part in range(2):
                to = (2 * term + part) * half
                keep_ref[to : to + half, cols] = rows[at : at + half].astype(BF)
                at += half + late
        high, low = rows[: 2 * (half + late)], rows[2 * (half + late) :]
        for part in range(2):
            at = part * (half + late) + half
            send_ref[part, :, cols] = high[at : at + late] + low[at : at + late]


def pick_early_kernel(start, turn, other_perm, *refs):
    *early, out_ref, _ = refs
    for cols in tiles(out_ref.shape[1]):
        where = slice(start + cols.start, start + cols.stop)
        out_ref[:, cols] = picked(other_perm[:, where], early, cols.stop - cols.start).astype(BF)


def switch_kernel(turn, w, keep_in, early_in, late_in, keep_ref, send_ref, next_turn):
    half, late = keep_ref.shape[1], late_in.shape[1]
    rest = half - late
    for cols in tiles(send_ref.shape[2]):
        late_terms = [split(late_in[part, :, cols]) for part in range(2)]
        z = []
        for term in range(2):
            rows = []
            for part in range(2):
                at = 2 * term + part
                rows.append(keep_in[at * half : (at + 1) * half, cols])
                rows.append(early_in[at * rest : (at + 1) * rest, cols])
                rows.append(late_terms[part][term])
            z.append(jnp.concatenate(rows, axis=0))
        put_halves(product(w, z), keep_ref, send_ref, cols)


def last_kernel(at, turn, w, c, measured_ref, keep_in, recv_in, *rest):
    out_ref, _, tile_ref, left = rest[-4:]
    copies = []
    for n, cols in enumerate(tiles(keep_in.shape[2])):
        z = split(stacked(keep_in[:, :, cols], recv_in[:, :, cols]))
        image = product(c, split(product(w, z)))
        half = image.shape[0] // 2
        re, im = image[:half], image[half:]
        scale = measured_ref[0, :, cols] * lax.rsqrt(jnp.maximum(re * re + im * im, 0.25))
        tile_ref[0, :, cols] = re * scale
        tile_ref[1, :, cols] = im * scale
        target = out_ref.at[0, :, :, pl.ds(at + cols.start, cols.stop - cols.start)]
        copies.append(pltpu.make_async_copy(tile_ref.at[:, :, cols], target, left.at[n]))
        copies[-1].start()
    for copy in copies:
        copy.wait()


def whole():
    return pl.BlockSpec(memory_space=pltpu.VMEM)


def anywhere():
    return pl.BlockSpec(memory_space=pl.ANY)


COST = pl.CostEstimate(flops=1000000000, bytes_accessed=2500000, transcendentals=0)


def per_device(wavefield, measured, leaf_map, factors, closing, box_perm, factor_order):
    _, _, cells, boxes = wavefield.shape
    level_count, slots = factors.shape[0], factors.shape[3]
    half = slots // 2
    late = half * LATE_ROWS // 64
    levels = levels_of(level_count, lax.axis_size("dev"))
    switch_at = level_count // 2
    first, second = cuts(FIRST_SIXTEENTHS, boxes), cuts(SECOND_SIXTEENTHS, boxes)
    params = pltpu.CompilerParams(vmem_limit_bytes=32 << 20)
    turn_shape = jax.ShapeDtypeStruct((8, 128), F32)
    turn = factor_order
    name = "product"

    def call(kernel, ins, args, shapes, **more):
        nonlocal turn, name
        *outs, turn = pl.pallas_call(
            kernel,
            in_specs=[anywhere(), *ins],
            out_specs=[*more.pop("outs", [whole()] * len(shapes)), anywhere()],
            out_shape=[*shapes, turn_shape],
            compiler_params=params,
            cost_estimate=COST,
            name=name,
            **more,
        )(turn, *args)
        return outs

    def halves(width):
        return [jax.ShapeDtypeStruct((2, half, width), F32)] * 2

    def leaf(parts, after):
        nonlocal turn
        stay = pl.BlockSpec(memory_space=pltpu.HBM)
        ins, args = [stay] * 2, [wavefield, leaf_map]
        kernel = functools.partial(leaf_kernel, levels[0], parts)
        if after:
            ins, args = [anywhere()] + ins, [turn] + args
            kernel = functools.partial(after_turn, kernel)
        *outs, turn = pl.pallas_call(
            kernel,
            in_specs=ins,
            out_specs=[*[whole()] * (2 * len(parts)), anywhere()],
            out_shape=[shape for part in parts for shape in halves(part[1])] + [turn_shape],
            scratch_shapes=[
                *[pltpu.VMEM((2, cells, part[1]), F32) for part in parts],
                pltpu.VMEM(leaf_map.shape, F32),
                pltpu.SemaphoreType.DMA((len(parts) + 1,)),
            ],
            compiler_params=pltpu.CompilerParams(vmem_limit_bytes=(32 if after else 61) << 20),
            cost_estimate=COST,
            name="leaf",
        )(*args)
        return list(zip(outs[::2], outs[1::2]))

    def prepared():
        matrix = jax.ShapeDtypeStruct((2, 2 * slots, 2 * slots), BF)
        shapes = [jax.ShapeDtypeStruct(box_perm.shape, box_perm.dtype)] + [matrix] * (level_count + 1)
        perm, closing_terms, *factor_terms = call(
            functools.partial(weights_kernel, levels),
            [pl.BlockSpec(memory_space=pltpu.SMEM)] + [whole()] * 3,
            [factor_order, factors, closing, box_perm],
            shapes,
        )
        return perm, closing_terms, factor_terms

    def terms_of(rows, width):
        return jax.ShapeDtypeStruct((4 * rows, width), BF)

    def block_of(rows, width):
        return jax.ShapeDtypeStruct((2, rows, width), F32)

    def level(w, keep, recv):
        return call(level_kernel, [whole()] * 3, [w, keep, recv], halves(recv.shape[2]))

    def ready(w, keep, recv, order):
        width, early = recv.shape[2], half - late + ORDER_ROWS * len(order)
        shapes = [terms_of(half + late, width), block_of(early, width)]
        args = [w, keep, recv, *order]
        return call(ready_kernel, [whole()] * len(args), args, shapes)

    def terms(block, order):
        shapes = [terms_of(half - late, block.shape[2])]
        return call(terms_kernel, [whole()], [block], shapes + order)

    def pick_own(part, own_perm, parts):
        at, width = part
        kernel = functools.partial(pick_own_kernel, at)
        shapes = [terms_of(half, width), block_of(late, width)]
        return call(kernel, [whole()] * (1 + len(parts)), [own_perm, *parts], shapes)

    def pick_early(part, order, parts):
        at, width = part
        kernel = functools.partial(pick_early_kernel, at)
        return call(kernel, [whole()] * (1 + len(parts)), [order, *parts], [terms_of(half - late, width)])[0]

    def switch(w, keep, early, late_rows):
        return call(switch_kernel, [whole()] * 4, [w, keep, early, late_rows], halves(late_rows.shape[2]))

    def last(part, w, c, keep, recv, so_far):
        at, width = part
        ins = [whole()] * 5
        args = [w, c, lax.slice_in_dim(measured, at, at + width, axis=2), keep, recv]
        aliases = {}
        if so_far is not None:
            ins.append(pl.BlockSpec(memory_space=pltpu.HBM))
            aliases = {len(args) + 1: 0}
            args.append(so_far)
        return call(
            functools.partial(last_kernel, at), ins, args,
            [jax.ShapeDtypeStruct((1, 2, cells, boxes), F32)],
            outs=[pl.BlockSpec(memory_space=pltpu.HBM)], input_output_aliases=aliases,
            scratch_shapes=[pltpu.VMEM((2, cells, width), F32), pltpu.SemaphoreType.DMA((len(tiles(width)),))],
        )[0]

    own, away = {}, {}

    def leave(part, step, keep, send):
        own[part], away[part] = keep, swapped(send, levels[step], f"send_{part}_{step}")

    first_leaf = leaf(first[:1], False)
    leaves = first_leaf + leaf(first[1:], True)
    name = "weights"
    own_perm, closing_terms, factor_terms = prepared()
    other_perm, arrived, early = [], [], {}

    def first_begin(part):
        leave(part, 0, *leaves[part])

    def first_step(part, step):
        nonlocal name
        name = f"part_{part}_{step}"
        w = factor_terms[step - 1]
        if step > switch_at:
            order = [jax.ShapeDtypeStruct(box_perm.shape, box_perm.dtype)] if part == 0 else []
            away[part], *other = terms(away[part], order)
            other_perm.extend(other)
            arrived.append(part)
            if len(arrived) == len(first):
                for waiting in sorted(own2):
                    gather(waiting)
        elif step == switch_at:
            order = [own_perm] if part == 0 else []
            leave(part, step, *ready(w, own[part], away[part], order))
        else:
            leave(part, step, *level(w, own[part], away[part]))

    def second_begin(part):
        nonlocal name
        name = f"again_{part}_{switch_at - 1}"
        kept = [own[n] for n in range(len(first))]
        keep, send = pick_own(second[part], own_perm, kept)
        own2[part], away2[part] = keep, swapped(send, levels[switch_at], f"send_{part}_late")
        if len(arrived) == len(first):
            gather(part)

    def gather(part):
        nonlocal name
        name = f"early_{part}"
        parts = [away[n] for n in range(len(first))]
        early[part] = pick_early(second[part], *other_perm, parts)

    def second_step(part, step):
        nonlocal name, out
        step += switch_at - 1
        name = f"again_{part}_{step}"
        w = factor_terms[step]
        if step == level_count - 1:
            out = last(second[part], w, closing_terms, own2[part], away2[part], out)
            return
        if step == switch_at:
            keep, send = switch(w, own2[part], early[part], away2[part])
        else:
            keep, send = level(w, own2[part], away2[part])
        own2[part], away2[part] = keep, swapped(send, levels[step + 1], f"send_{part}_{step + 1}")

    own2, away2, out = {}, {}, None
    in_turn(
        (FIRST_STARTS, switch_at + 1, first_begin, first_step),
        (SECOND_STARTS, level_count - switch_at, second_begin, second_step),
    )
    return out


def solution(mesh):
    return jax.shard_map(
        per_device,
        mesh=mesh,
        in_specs=(
            P(("grp", "dev"), None, None, None),
            P(("grp", "dev"), None, None),
            P(("grp", "dev"), None, None, None),
            P(None, ("grp", "dev"), None, None, None),
            P(("grp", "dev"), None, None, None),
            P(("grp", "dev"), None),
            P(),
        ),
        out_specs=P(("grp", "dev"), None, None, None),
        check_vma=False,
    )
```

```python
import functools

import jax
import jax.numpy as jnp
from jax import lax
from jax.experimental import pallas as pl
from jax.experimental.pallas import tpu as pltpu
from jax.sharding import PartitionSpec as P

BF = jnp.bfloat16
F32 = jnp.float32
FIRST_SIXTEENTHS = (3, 3, 4, 4, 2)
SECOND_SIXTEENTHS = (3, 3, 4, 4, 2)
FIRST_STARTS = (0, 0, 1, 3, 6)
SECOND_STARTS = (0, 1, 3, 5, 8)
LATE_ROWS = 32
ORDER_ROWS = 8
TILE = 512


def levels_of(level_count, dev_size):
    dev_bits = dev_size.bit_length() - 1
    return [
        ("grp", 1 - j) if j < 2 else ("dev", (j - 2) % dev_bits)
        for j in range(level_count)
    ]


def swapped(block, level, name):
    axis, bit = level
    count = lax.axis_size(axis)
    with jax.named_scope(name):
        return lax.ppermute(block, axis, [(i, i ^ 1 << bit) for i in range(count)])


def half_bit(level):
    return lax.axis_index(level[0]) >> level[1] & 1


def cuts(sixteenths, boxes):
    unit = boxes // 16
    parts, at = [], 0
    for share in sixteenths:
        parts.append((at, share * unit))
        at += share * unit
    return parts


def split(values):
    high = values.astype(BF)
    return high, (values - high.astype(F32)).astype(BF)


def weights(re, im, column_bit, row_bit):
    def ordered(part):
        half = part.shape[0] // 2
        if column_bit is not None:
            turned = jnp.concatenate([part[:, half:], part[:, :half]], axis=1)
            part = jnp.where(column_bit == 1, turned, part)
        if row_bit is not None:
            turned = jnp.concatenate([part[half:], part[:half]], axis=0)
            part = jnp.where(row_bit == 1, turned, part)
        return part

    re, im = ordered(re), ordered(im)
    return split(
        jnp.concatenate(
            [jnp.concatenate([re, -im], axis=1), jnp.concatenate([im, re], axis=1)],
            axis=0,
        )
    )


def dot(a, b):
    return jnp.dot(a, b, preferred_element_type=F32)


def product(w, z):
    return dot(w[0], z[0]) + (dot(w[0], z[1]) + dot(w[1], z[0]))


def tiles(width):
    step = min(TILE, width)
    return [slice(at, min(at + step, width)) for at in range(0, width, step)]


def put_halves(result, keep_ref, send_ref, cols):
    half = result.shape[0] // 4
    for part in range(2):
        keep_ref[part, :, cols] = result[2 * part * half : (2 * part + 1) * half]
        send_ref[part, :, cols] = result[(2 * part + 1) * half : (2 * part + 2) * half]


def stacked(keep, recv):
    return jnp.concatenate([keep[0], recv[0], keep[1], recv[1]], axis=0)


def in_turn(first, second):
    pending, used, begun, ready = [], [0, 0], [0, 0], 0
    phases = (first, second)
    while pending or begun[1] < len(second[0]):
        for phase, (starts, _, begin, _) in enumerate(phases):
            part = begun[phase]
            open_now = phase == 0 or ready == len(first[0])
            if part < len(starts) and open_now and (used[phase] >= starts[part] or not pending):
                begin(part)
                pending.append((phase, part, 1))
                begun[phase] += 1
                break
        else:
            phase, part, step = pending.pop(0)
            _, steps, _, go_on = phases[phase]
            used = [used[0] + 1, used[1] + (ready == len(first[0]))]
            go_on(part, step)
            ready += phase == 0 and step == steps - 1
            if step < steps:
                pending.append((phase, part, step + 1))


def leaf_kernel(level, parts, field_ref, leaf_ref, *refs):
    count = len(parts)
    outs, turn, rest = refs[: 2 * count], refs[2 * count], refs[2 * count + 1 :]
    fields, leaf, arrived = rest[:count], rest[count], rest[count + 1]
    copies = [pltpu.make_async_copy(leaf_ref, leaf, arrived.at[count])]
    for n, (at, width) in enumerate(parts):
        source = field_ref.at[0, :, :, pl.ds(at, width)]
        copies.append(pltpu.make_async_copy(source, fields[n], arrived.at[n]))
    for copy in copies:
        copy.start()
    copies[0].wait()
    w = weights(leaf[0, 0], leaf[0, 1], None, half_bit(level))
    for n in range(count):
        copies[n + 1].wait()
        for cols in tiles(parts[n][1]):
            field = fields[n][:, :, cols]
            z = split(field.reshape(-1, field.shape[-1]))
            put_halves(product(w, z), outs[2 * n], outs[2 * n + 1], cols)


def after_turn(kernel, turn, *refs):
    kernel(*refs)


def weights_kernel(levels, turn, order_ref, factors_ref, closing_ref, perm_ref, *outs):
    perm_out, closing_out, *factor_outs, next_turn = outs
    perm_out[...] = perm_ref[...]
    for j, out in enumerate(factor_outs):
        at = order_ref[j]
        following = half_bit(levels[j + 1]) if j + 1 < len(levels) else None
        high, low = weights(factors_ref[at, 0, 0], factors_ref[at, 0, 1], half_bit(levels[j]), following)
        out[0], out[1] = high, low
    closing_out[0], closing_out[1] = weights(closing_ref[0, 0], closing_ref[0, 1], None, None)


def put_terms(values, out_ref, cols):
    at = 0
    for terms in zip(*(split(value) for value in values)):
        for term in terms:
            out_ref[at : at + term.shape[0], cols] = term
            at += term.shape[0]


def level_kernel(turn, w, keep_in, recv_in, keep_ref, send_ref, next_turn):
    for cols in tiles(send_ref.shape[2]):
        z = split(stacked(keep_in[:, :, cols], recv_in[:, :, cols]))
        put_halves(product(w, z), keep_ref, send_ref, cols)


def ready_kernel(turn, w, keep_in, recv_in, *refs):
    own_ref, send_ref, _ = refs[-3:]
    early = send_ref.shape[1]
    if len(refs) > 3:
        early -= ORDER_ROWS
        put_order(refs[0], send_ref, early)
    for cols in tiles(send_ref.shape[2]):
        z = split(stacked(keep_in[:, :, cols], recv_in[:, :, cols]))
        result = product(w, z)
        slots = result.shape[0] // 2
        half = slots // 2
        own = []
        for part in range(2):
            rows = result[part * slots : (part + 1) * slots]
            own.append(jnp.concatenate([rows[:half], rows[half + early :]], axis=0))
            send_ref[part, :early, cols] = rows[half : half + early]
        put_terms(own, own_ref, cols)


def order_places(boxes, width):
    places = [(n // ORDER_ROWS, n % ORDER_ROWS, n * width) for n in range(-(-boxes // width))]
    return [(part, row, slice(at, min(at + width, boxes))) for part, row, at in places]


def put_order(perm_ref, send_ref, early):
    boxes, width = perm_ref.shape[1], send_ref.shape[2]
    blank = jnp.zeros((1, width), F32)
    rows = [[blank] * ORDER_ROWS for _ in range(2)]
    for part, row, where in order_places(boxes, width):
        here = perm_ref[:, where].astype(F32)
        if here.shape[1] < width:
            here = jnp.concatenate([here, blank[:, here.shape[1] :]], axis=1)
        rows[part][row] = here
    for part in range(2):
        send_ref[part, early:] = jnp.concatenate(rows[part], axis=0)


def terms_kernel(turn, part_ref, out_ref, *rest):
    early = out_ref.shape[0] // 4
    for cols in tiles(part_ref.shape[2]):
        put_terms([part_ref[part, :early, cols] for part in range(2)], out_ref, cols)
    if len(rest) > 1:
        perm_ref = rest[0]
        for part, row, where in order_places(perm_ref.shape[1], part_ref.shape[2]):
            width = where.stop - where.start
            here = part_ref[part, early + row : early + row + 1, :width]
            perm_ref[:, where] = here.astype(jnp.int32)


def picked(perm, parts, width):
    total, at = None, 0
    for part in parts:
        for rows in tiles(part.shape[1]):
            depth = rows.stop - rows.start
            box = lax.broadcasted_iota(jnp.int32, (depth, width), 0) + at
            chosen = jnp.where(box == perm, 1.0, 0.0).astype(BF)
            here = dot(part[:, rows], chosen)
            total = here if total is None else total + here
            at += depth
    return total


def pick_own_kernel(start, turn, own_perm, *refs):
    *own, keep_ref, send_ref, _ = refs
    half, late = keep_ref.shape[0] // 4, send_ref.shape[1]
    for cols in tiles(send_ref.shape[2]):
        where = slice(start + cols.start, start + cols.stop)
        rows = picked(own_perm[:, where], own, cols.stop - cols.start)
        at = 0
        for term in range(2):
            for part in range(2):
                to = (2 * term + part) * half
                keep_ref[to : to + half, cols] = rows[at : at + half].astype(BF)
                at += half + late
        high, low = rows[: 2 * (half + late)], rows[2 * (half + late) :]
        for part in range(2):
            at = part * (half + late) + half
            send_ref[part, :, cols] = high[at : at + late] + low[at : at + late]


def pick_early_kernel(start, turn, other_perm, *refs):
    *early, out_ref, _ = refs
    for cols in tiles(out_ref.shape[1]):
        where = slice(start + cols.start, start + cols.stop)
        out_ref[:, cols] = picked(other_perm[:, where], early, cols.stop - cols.start).astype(BF)


def switch_kernel(turn, w, keep_in, early_in, late_in, keep_ref, send_ref, next_turn):
    half, late = keep_ref.shape[1], late_in.shape[1]
    rest = half - late
    for cols in tiles(send_ref.shape[2]):
        late_terms = [split(late_in[part, :, cols]) for part in range(2)]
        z = []
        for term in range(2):
            rows = []
            for part in range(2):
                at = 2 * term + part
                rows.append(keep_in[at * half : (at + 1) * half, cols])
                rows.append(early_in[at * rest : (at + 1) * rest, cols])
                rows.append(late_terms[part][term])
            z.append(jnp.concatenate(rows, axis=0))
        put_halves(product(w, z), keep_ref, send_ref, cols)


def last_kernel(at, turn, w, c, measured_ref, keep_in, recv_in, *rest):
    out_ref, _, tile_ref, left = rest[-4:]
    copies = []
    for n, cols in enumerate(tiles(keep_in.shape[2])):
        z = split(stacked(keep_in[:, :, cols], recv_in[:, :, cols]))
        image = product(c, split(product(w, z)))
        half = image.shape[0] // 2
        re, im = image[:half], image[half:]
        scale = measured_ref[0, :, cols] * lax.rsqrt(jnp.maximum(re * re + im * im, 0.25))
        tile_ref[0, :, cols] = re * scale
        tile_ref[1, :, cols] = im * scale
        target = out_ref.at[0, :, :, pl.ds(at + cols.start, cols.stop - cols.start)]
        copies.append(pltpu.make_async_copy(tile_ref.at[:, :, cols], target, left.at[n]))
        copies[-1].start()
    for copy in copies:
        copy.wait()


def whole():
    return pl.BlockSpec(memory_space=pltpu.VMEM)


def anywhere():
    return pl.BlockSpec(memory_space=pl.ANY)


COST = pl.CostEstimate(flops=1000000000, bytes_accessed=2500000, transcendentals=0)


def per_device(wavefield, measured, leaf_map, factors, closing, box_perm, factor_order):
    _, _, cells, boxes = wavefield.shape
    level_count, slots = factors.shape[0], factors.shape[3]
    half = slots // 2
    late = half * LATE_ROWS // 64
    levels = levels_of(level_count, lax.axis_size("dev"))
    switch_at = level_count // 2
    first, second = cuts(FIRST_SIXTEENTHS, boxes), cuts(SECOND_SIXTEENTHS, boxes)
    params = pltpu.CompilerParams(vmem_limit_bytes=32 << 20)
    turn_shape = jax.ShapeDtypeStruct((8, 128), F32)
    turn = factor_order
    name = "product"

    def call(kernel, ins, args, shapes, **more):
        nonlocal turn, name
        *outs, turn = pl.pallas_call(
            kernel,
            in_specs=[anywhere(), *ins],
            out_specs=[*more.pop("outs", [whole()] * len(shapes)), anywhere()],
            out_shape=[*shapes, turn_shape],
            compiler_params=params,
            cost_estimate=COST,
            name=name,
            **more,
        )(turn, *args)
        return outs

    def halves(width):
        return [jax.ShapeDtypeStruct((2, half, width), F32)] * 2

    def leaf(parts, after):
        nonlocal turn
        stay = pl.BlockSpec(memory_space=pltpu.HBM)
        ins, args = [stay] * 2, [wavefield, leaf_map]
        kernel = functools.partial(leaf_kernel, levels[0], parts)
        if after:
            ins, args = [anywhere()] + ins, [turn] + args
            kernel = functools.partial(after_turn, kernel)
        *outs, turn = pl.pallas_call(
            kernel,
            in_specs=ins,
            out_specs=[*[whole()] * (2 * len(parts)), anywhere()],
            out_shape=[shape for part in parts for shape in halves(part[1])] + [turn_shape],
            scratch_shapes=[
                *[pltpu.VMEM((2, cells, part[1]), F32) for part in parts],
                pltpu.VMEM(leaf_map.shape, F32),
                pltpu.SemaphoreType.DMA((len(parts) + 1,)),
            ],
            compiler_params=pltpu.CompilerParams(vmem_limit_bytes=(32 if after else 61) << 20),
            cost_estimate=COST,
            name="leaf",
        )(*args)
        return list(zip(outs[::2], outs[1::2]))

    def prepared():
        matrix = jax.ShapeDtypeStruct((2, 2 * slots, 2 * slots), BF)
        shapes = [jax.ShapeDtypeStruct(box_perm.shape, box_perm.dtype)] + [matrix] * (level_count + 1)
        perm, closing_terms, *factor_terms = call(
            functools.partial(weights_kernel, levels),
            [pl.BlockSpec(memory_space=pltpu.SMEM)] + [whole()] * 3,
            [factor_order, factors, closing, box_perm],
            shapes,
        )
        return perm, closing_terms, factor_terms

    def terms_of(rows, width):
        return jax.ShapeDtypeStruct((4 * rows, width), BF)

    def block_of(rows, width):
        return jax.ShapeDtypeStruct((2, rows, width), F32)

    def level(w, keep, recv):
        return call(level_kernel, [whole()] * 3, [w, keep, recv], halves(recv.shape[2]))

    def ready(w, keep, recv, order):
        width, early = recv.shape[2], half - late + ORDER_ROWS * len(order)
        shapes = [terms_of(half + late, width), block_of(early, width)]
        args = [w, keep, recv, *order]
        return call(ready_kernel, [whole()] * len(args), args, shapes)

    def terms(block, order):
        shapes = [terms_of(half - late, block.shape[2])]
        return call(terms_kernel, [whole()], [block], shapes + order)

    def pick_own(part, own_perm, parts):
        at, width = part
        kernel = functools.partial(pick_own_kernel, at)
        shapes = [terms_of(half, width), block_of(late, width)]
        return call(kernel, [whole()] * (1 + len(parts)), [own_perm, *parts], shapes)

    def pick_early(part, order, parts):
        at, width = part
        kernel = functools.partial(pick_early_kernel, at)
        return call(kernel, [whole()] * (1 + len(parts)), [order, *parts], [terms_of(half - late, width)])[0]

    def switch(w, keep, early, late_rows):
        return call(switch_kernel, [whole()] * 4, [w, keep, early, late_rows], halves(late_rows.shape[2]))

    def last(part, w, c, keep, recv, so_far):
        at, width = part
        ins = [whole()] * 5
        args = [w, c, lax.slice_in_dim(measured, at, at + width, axis=2), keep, recv]
        aliases = {}
        if so_far is not None:
            ins.append(pl.BlockSpec(memory_space=pltpu.HBM))
            aliases = {len(args) + 1: 0}
            args.append(so_far)
        return call(
            functools.partial(last_kernel, at), ins, args,
            [jax.ShapeDtypeStruct((1, 2, cells, boxes), F32)],
            outs=[pl.BlockSpec(memory_space=pltpu.HBM)], input_output_aliases=aliases,
            scratch_shapes=[pltpu.VMEM((2, cells, width), F32), pltpu.SemaphoreType.DMA((len(tiles(width)),))],
        )[0]

    own, away = {}, {}

    def leave(part, step, keep, send):
        own[part], away[part] = keep, swapped(send, levels[step], f"send_{part}_{step}")

    first_leaf = leaf(first[:1], False)
    leaves = first_leaf + leaf(first[1:], True)
    name = "weights"
    own_perm, closing_terms, factor_terms = prepared()
    other_perm, arrived, early = [], [], {}

    def first_begin(part):
        leave(part, 0, *leaves[part])

    def first_step(part, step):
        nonlocal name
        name = f"part_{part}_{step}"
        w = factor_terms[step - 1]
        if step > switch_at:
            order = [jax.ShapeDtypeStruct(box_perm.shape, box_perm.dtype)] if part == 0 else []
            away[part], *other = terms(away[part], order)
            other_perm.extend(other)
            arrived.append(part)
            if len(arrived) == len(first):
                for waiting in sorted(own2):
                    gather(waiting)
        elif step == switch_at:
            order = [own_perm] if part == 0 else []
            leave(part, step, *ready(w, own[part], away[part], order))
        else:
            leave(part, step, *level(w, own[part], away[part]))

    def second_begin(part):
        nonlocal name
        name = f"again_{part}_{switch_at - 1}"
        kept = [own[n] for n in range(len(first))]
        keep, send = pick_own(second[part], own_perm, kept)
        own2[part], away2[part] = keep, swapped(send, levels[switch_at], f"send_{part}_late")
        if len(arrived) == len(first):
            gather(part)

    def gather(part):
        nonlocal name
        name = f"early_{part}"
        parts = [away[n] for n in range(len(first))]
        early[part] = pick_early(second[part], *other_perm, parts)

    def second_step(part, step):
        nonlocal name, out
        step += switch_at - 1
        name = f"again_{part}_{step}"
        w = factor_terms[step]
        if step == level_count - 1:
            out = last(second[part], w, closing_terms, own2[part], away2[part], out)
            return
        if step == switch_at:
            keep, send = switch(w, own2[part], early[part], away2[part])
        else:
            keep, send = level(w, own2[part], away2[part])
        own2[part], away2[part] = keep, swapped(send, levels[step + 1], f"send_{part}_{step + 1}")

    own2, away2, out = {}, {}, None
    in_turn(
        (FIRST_STARTS, switch_at + 1, first_begin, first_step),
        (SECOND_STARTS, level_count - switch_at, second_begin, second_step),
    )
    return out


def solution(mesh):
    return jax.shard_map(
        per_device,
        mesh=mesh,
        in_specs=(
            P(("grp", "dev"), None, None, None),
            P(("grp", "dev"), None, None),
            P(("grp", "dev"), None, None, None),
            P(None, ("grp", "dev"), None, None, None),
            P(("grp", "dev"), None, None, None),
            P(("grp", "dev"), None),
            P(),
        ),
        out_specs=P(("grp", "dev"), None, None, None),
        check_vma=False,
    )
```

```python
import functools

import jax
import jax.numpy as jnp
from jax import lax
from jax.experimental import pallas as pl
from jax.experimental.pallas import tpu as pltpu
from jax.sharding import PartitionSpec as P

BF = jnp.bfloat16
F32 = jnp.float32
FIRST_SIXTEENTHS = (3, 3, 4, 4, 2)
SECOND_SIXTEENTHS = (3, 3, 4, 4, 2)
FIRST_STARTS = (0, 0, 1, 3, 6)
SECOND_STARTS = (0, 1, 3, 5, 8)
LATE_ROWS = 32
ORDER_ROWS = 8
TILE = 512
LEAVING = 256


def levels_of(level_count, dev_size):
    dev_bits = dev_size.bit_length() - 1
    return [
        ("grp", 1 - j) if j < 2 else ("dev", (j - 2) % dev_bits)
        for j in range(level_count)
    ]


def swapped(block, level, name):
    axis, bit = level
    count = lax.axis_size(axis)
    with jax.named_scope(name):
        return lax.ppermute(block, axis, [(i, i ^ 1 << bit) for i in range(count)])


def half_bit(level):
    return lax.axis_index(level[0]) >> level[1] & 1


def cuts(sixteenths, boxes):
    unit = boxes // 16
    parts, at = [], 0
    for share in sixteenths:
        parts.append((at, share * unit))
        at += share * unit
    return parts


def split(values):
    high = values.astype(BF)
    return high, (values - high.astype(F32)).astype(BF)


def weights(re, im, column_bit, row_bit):
    def ordered(part):
        half = part.shape[0] // 2
        if column_bit is not None:
            turned = jnp.concatenate([part[:, half:], part[:, :half]], axis=1)
            part = jnp.where(column_bit == 1, turned, part)
        if row_bit is not None:
            turned = jnp.concatenate([part[half:], part[:half]], axis=0)
            part = jnp.where(row_bit == 1, turned, part)
        return part

    re, im = ordered(re), ordered(im)
    return split(
        jnp.concatenate(
            [jnp.concatenate([re, -im], axis=1), jnp.concatenate([im, re], axis=1)],
            axis=0,
        )
    )


def dot(a, b):
    return jnp.dot(a, b, preferred_element_type=F32)


def product(w, z):
    return dot(w[0], z[0]) + (dot(w[0], z[1]) + dot(w[1], z[0]))


def tiles(width, limit=TILE):
    step = min(limit, width)
    return [slice(at, min(at + step, width)) for at in range(0, width, step)]


def put_halves(result, keep_ref, send_ref, cols):
    half = result.shape[0] // 4
    for part in range(2):
        keep_ref[part, :, cols] = result[2 * part * half : (2 * part + 1) * half]
        send_ref[part, :, cols] = result[(2 * part + 1) * half : (2 * part + 2) * half]


def stacked(keep, recv):
    return jnp.concatenate([keep[0], recv[0], keep[1], recv[1]], axis=0)


def in_turn(first, second):
    pending, used, begun, ready = [], [0, 0], [0, 0], 0
    phases = (first, second)
    while pending or begun[1] < len(second[0]):
        for phase, (starts, _, begin, _) in enumerate(phases):
            part = begun[phase]
            open_now = phase == 0 or ready == len(first[0])
            if part < len(starts) and open_now and (used[phase] >= starts[part] or not pending):
                begin(part)
                pending.append((phase, part, 1))
                begun[phase] += 1
                break
        else:
            phase, part, step = pending.pop(0)
            _, steps, _, go_on = phases[phase]
            used = [used[0] + 1, used[1] + (ready == len(first[0]))]
            go_on(part, step)
            ready += phase == 0 and step == steps - 1
            if step < steps:
                pending.append((phase, part, step + 1))


def leaf_kernel(level, parts, field_ref, leaf_ref, *refs):
    count = len(parts)
    outs, turn, rest = refs[: 2 * count], refs[2 * count], refs[2 * count + 1 :]
    fields, leaf, arrived = rest[:count], rest[count], rest[count + 1]
    copies = [pltpu.make_async_copy(leaf_ref, leaf, arrived.at[count])]
    for n, (at, width) in enumerate(parts):
        source = field_ref.at[0, :, :, pl.ds(at, width)]
        copies.append(pltpu.make_async_copy(source, fields[n], arrived.at[n]))
    for copy in copies:
        copy.start()
    copies[0].wait()
    w = weights(leaf[0, 0], leaf[0, 1], None, half_bit(level))
    for n in range(count):
        copies[n + 1].wait()
        for cols in tiles(parts[n][1]):
            field = fields[n][:, :, cols]
            z = split(field.reshape(-1, field.shape[-1]))
            put_halves(product(w, z), outs[2 * n], outs[2 * n + 1], cols)


def after_turn(kernel, turn, *refs):
    kernel(*refs)


def weights_kernel(levels, turn, order_ref, factors_ref, closing_ref, perm_ref, *outs):
    perm_out, closing_out, *factor_outs, next_turn = outs
    perm_out[...] = perm_ref[...]
    for j, out in enumerate(factor_outs):
        at = order_ref[j]
        following = half_bit(levels[j + 1]) if j + 1 < len(levels) else None
        high, low = weights(factors_ref[at, 0, 0], factors_ref[at, 0, 1], half_bit(levels[j]), following)
        out[0], out[1] = high, low
    closing_out[0], closing_out[1] = weights(closing_ref[0, 0], closing_ref[0, 1], None, None)


def put_terms(values, out_ref, cols):
    at = 0
    for terms in zip(*(split(value) for value in values)):
        for term in terms:
            out_ref[at : at + term.shape[0], cols] = term
            at += term.shape[0]


def level_kernel(turn, w, keep_in, recv_in, keep_ref, send_ref, next_turn):
    for cols in tiles(send_ref.shape[2]):
        z = split(stacked(keep_in[:, :, cols], recv_in[:, :, cols]))
        put_halves(product(w, z), keep_ref, send_ref, cols)


def ready_kernel(turn, w, keep_in, recv_in, *refs):
    own_ref, send_ref, _ = refs[-3:]
    early = send_ref.shape[1]
    if len(refs) > 3:
        early -= ORDER_ROWS
        put_order(refs[0], send_ref, early)
    for cols in tiles(send_ref.shape[2]):
        z = split(stacked(keep_in[:, :, cols], recv_in[:, :, cols]))
        result = product(w, z)
        slots = result.shape[0] // 2
        half = slots // 2
        own = []
        for part in range(2):
            rows = result[part * slots : (part + 1) * slots]
            own.append(jnp.concatenate([rows[:half], rows[half + early :]], axis=0))
            send_ref[part, :early, cols] = rows[half : half + early]
        put_terms(own, own_ref, cols)


def order_places(boxes, width):
    places = [(n // ORDER_ROWS, n % ORDER_ROWS, n * width) for n in range(-(-boxes // width))]
    return [(part, row, slice(at, min(at + width, boxes))) for part, row, at in places]


def put_order(perm_ref, send_ref, early):
    boxes, width = perm_ref.shape[1], send_ref.shape[2]
    blank = jnp.zeros((1, width), F32)
    rows = [[blank] * ORDER_ROWS for _ in range(2)]
    for part, row, where in order_places(boxes, width):
        here = perm_ref[:, where].astype(F32)
        if here.shape[1] < width:
            here = jnp.concatenate([here, blank[:, here.shape[1] :]], axis=1)
        rows[part][row] = here
    for part in range(2):
        send_ref[part, early:] = jnp.concatenate(rows[part], axis=0)


def terms_kernel(turn, part_ref, out_ref, *rest):
    early = out_ref.shape[0] // 4
    for cols in tiles(part_ref.shape[2]):
        put_terms([part_ref[part, :early, cols] for part in range(2)], out_ref, cols)
    if len(rest) > 1:
        perm_ref = rest[0]
        for part, row, where in order_places(perm_ref.shape[1], part_ref.shape[2]):
            width = where.stop - where.start
            here = part_ref[part, early + row : early + row + 1, :width]
            perm_ref[:, where] = here.astype(jnp.int32)


def picked(perm, parts, width):
    total, at = None, 0
    for part in parts:
        for rows in tiles(part.shape[1]):
            depth = rows.stop - rows.start
            box = lax.broadcasted_iota(jnp.int32, (depth, width), 0) + at
            chosen = jnp.where(box == perm, 1.0, 0.0).astype(BF)
            here = dot(part[:, rows], chosen)
            total = here if total is None else total + here
            at += depth
    return total


def pick_own_kernel(start, turn, own_perm, *refs):
    *own, keep_ref, send_ref, _ = refs
    half, late = keep_ref.shape[0] // 4, send_ref.shape[1]
    for cols in tiles(send_ref.shape[2]):
        where = slice(start + cols.start, start + cols.stop)
        rows = picked(own_perm[:, where], own, cols.stop - cols.start)
        at = 0
        for term in range(2):
            for part in range(2):
                to = (2 * term + part) * half
                keep_ref[to : to + half, cols] = rows[at : at + half].astype(BF)
                at += half + late
        high, low = rows[: 2 * (half + late)], rows[2 * (half + late) :]
        for part in range(2):
            at = part * (half + late) + half
            send_ref[part, :, cols] = high[at : at + late] + low[at : at + late]


def pick_early_kernel(start, turn, other_perm, *refs):
    *early, out_ref, _ = refs
    for cols in tiles(out_ref.shape[1]):
        where = slice(start + cols.start, start + cols.stop)
        out_ref[:, cols] = picked(other_perm[:, where], early, cols.stop - cols.start).astype(BF)


def switch_kernel(turn, w, keep_in, early_in, late_in, keep_ref, send_ref, next_turn):
    half, late = keep_ref.shape[1], late_in.shape[1]
    rest = half - late
    for cols in tiles(send_ref.shape[2]):
        late_terms = [split(late_in[part, :, cols]) for part in range(2)]
        z = []
        for term in range(2):
            rows = []
            for part in range(2):
                at = 2 * term + part
                rows.append(keep_in[at * half : (at + 1) * half, cols])
                rows.append(early_in[at * rest : (at + 1) * rest, cols])
                rows.append(late_terms[part][term])
            z.append(jnp.concatenate(rows, axis=0))
        put_halves(product(w, z), keep_ref, send_ref, cols)


def last_kernel(at, turn, w, c, measured_ref, keep_in, recv_in, *rest):
    out_ref, _, tile_ref, left = rest[-4:]
    copies = []
    for n, cols in enumerate(tiles(keep_in.shape[2], LEAVING)):
        z = split(stacked(keep_in[:, :, cols], recv_in[:, :, cols]))
        image = product(c, split(product(w, z)))
        half = image.shape[0] // 2
        re, im = image[:half], image[half:]
        scale = measured_ref[0, :, cols] * lax.rsqrt(jnp.maximum(re * re + im * im, 0.25))
        tile_ref[0, :, cols] = re * scale
        tile_ref[1, :, cols] = im * scale
        target = out_ref.at[0, :, :, pl.ds(at + cols.start, cols.stop - cols.start)]
        copies.append(pltpu.make_async_copy(tile_ref.at[:, :, cols], target, left.at[n]))
        copies[-1].start()
    for copy in copies:
        copy.wait()


def whole():
    return pl.BlockSpec(memory_space=pltpu.VMEM)


def anywhere():
    return pl.BlockSpec(memory_space=pl.ANY)


COST = pl.CostEstimate(flops=1000000000, bytes_accessed=2500000, transcendentals=0)


def per_device(wavefield, measured, leaf_map, factors, closing, box_perm, factor_order):
    _, _, cells, boxes = wavefield.shape
    level_count, slots = factors.shape[0], factors.shape[3]
    half = slots // 2
    late = half * LATE_ROWS // 64
    levels = levels_of(level_count, lax.axis_size("dev"))
    switch_at = level_count // 2
    first, second = cuts(FIRST_SIXTEENTHS, boxes), cuts(SECOND_SIXTEENTHS, boxes)
    params = pltpu.CompilerParams(vmem_limit_bytes=32 << 20)
    turn_shape = jax.ShapeDtypeStruct((8, 128), F32)
    turn = factor_order
    name = "product"

    def call(kernel, ins, args, shapes, **more):
        nonlocal turn, name
        *outs, turn = pl.pallas_call(
            kernel,
            in_specs=[anywhere(), *ins],
            out_specs=[*more.pop("outs", [whole()] * len(shapes)), anywhere()],
            out_shape=[*shapes, turn_shape],
            compiler_params=params,
            cost_estimate=COST,
            name=name,
            **more,
        )(turn, *args)
        return outs

    def halves(width):
        return [jax.ShapeDtypeStruct((2, half, width), F32)] * 2

    def leaf(parts, after):
        nonlocal turn
        stay = pl.BlockSpec(memory_space=pltpu.HBM)
        ins, args = [stay] * 2, [wavefield, leaf_map]
        kernel = functools.partial(leaf_kernel, levels[0], parts)
        if after:
            ins, args = [anywhere()] + ins, [turn] + args
            kernel = functools.partial(after_turn, kernel)
        *outs, turn = pl.pallas_call(
            kernel,
            in_specs=ins,
            out_specs=[*[whole()] * (2 * len(parts)), anywhere()],
            out_shape=[shape for part in parts for shape in halves(part[1])] + [turn_shape],
            scratch_shapes=[
                *[pltpu.VMEM((2, cells, part[1]), F32) for part in parts],
                pltpu.VMEM(leaf_map.shape, F32),
                pltpu.SemaphoreType.DMA((len(parts) + 1,)),
            ],
            compiler_params=pltpu.CompilerParams(vmem_limit_bytes=(32 if after else 61) << 20),
            cost_estimate=COST,
            name="leaf",
        )(*args)
        return list(zip(outs[::2], outs[1::2]))

    def prepared():
        matrix = jax.ShapeDtypeStruct((2, 2 * slots, 2 * slots), BF)
        shapes = [jax.ShapeDtypeStruct(box_perm.shape, box_perm.dtype)] + [matrix] * (level_count + 1)
        perm, closing_terms, *factor_terms = call(
            functools.partial(weights_kernel, levels),
            [pl.BlockSpec(memory_space=pltpu.SMEM)] + [whole()] * 3,
            [factor_order, factors, closing, box_perm],
            shapes,
        )
        return perm, closing_terms, factor_terms

    def terms_of(rows, width):
        return jax.ShapeDtypeStruct((4 * rows, width), BF)

    def block_of(rows, width):
        return jax.ShapeDtypeStruct((2, rows, width), F32)

    def level(w, keep, recv):
        return call(level_kernel, [whole()] * 3, [w, keep, recv], halves(recv.shape[2]))

    def ready(w, keep, recv, order):
        width, early = recv.shape[2], half - late + ORDER_ROWS * len(order)
        shapes = [terms_of(half + late, width), block_of(early, width)]
        args = [w, keep, recv, *order]
        return call(ready_kernel, [whole()] * len(args), args, shapes)

    def terms(block, order):
        shapes = [terms_of(half - late, block.shape[2])]
        return call(terms_kernel, [whole()], [block], shapes + order)

    def pick_own(part, own_perm, parts):
        at, width = part
        kernel = functools.partial(pick_own_kernel, at)
        shapes = [terms_of(half, width), block_of(late, width)]
        return call(kernel, [whole()] * (1 + len(parts)), [own_perm, *parts], shapes)

    def pick_early(part, order, parts):
        at, width = part
        kernel = functools.partial(pick_early_kernel, at)
        return call(kernel, [whole()] * (1 + len(parts)), [order, *parts], [terms_of(half - late, width)])[0]

    def switch(w, keep, early, late_rows):
        return call(switch_kernel, [whole()] * 4, [w, keep, early, late_rows], halves(late_rows.shape[2]))

    def last(part, w, c, keep, recv, so_far):
        at, width = part
        ins = [whole()] * 5
        args = [w, c, lax.slice_in_dim(measured, at, at + width, axis=2), keep, recv]
        aliases = {}
        if so_far is not None:
            ins.append(pl.BlockSpec(memory_space=pltpu.HBM))
            aliases = {len(args) + 1: 0}
            args.append(so_far)
        return call(
            functools.partial(last_kernel, at), ins, args,
            [jax.ShapeDtypeStruct((1, 2, cells, boxes), F32)],
            outs=[pl.BlockSpec(memory_space=pltpu.HBM)], input_output_aliases=aliases,
            scratch_shapes=[pltpu.VMEM((2, cells, width), F32), pltpu.SemaphoreType.DMA((len(tiles(width, LEAVING)),))],
        )[0]

    own, away = {}, {}

    def leave(part, step, keep, send):
        own[part], away[part] = keep, swapped(send, levels[step], f"send_{part}_{step}")

    first_leaf = leaf(first[:1], False)
    leaves = first_leaf + leaf(first[1:], True)
    name = "weights"
    own_perm, closing_terms, factor_terms = prepared()
    other_perm, arrived, early = [], [], {}

    def first_begin(part):
        leave(part, 0, *leaves[part])

    def first_step(part, step):
        nonlocal name
        name = f"part_{part}_{step}"
        w = factor_terms[step - 1]
        if step > switch_at:
            order = [jax.ShapeDtypeStruct(box_perm.shape, box_perm.dtype)] if part == 0 else []
            away[part], *other = terms(away[part], order)
            other_perm.extend(other)
            arrived.append(part)
            if len(arrived) == len(first):
                for waiting in sorted(own2):
                    gather(waiting)
        elif step == switch_at:
            order = [own_perm] if part == 0 else []
            leave(part, step, *ready(w, own[part], away[part], order))
        else:
            leave(part, step, *level(w, own[part], away[part]))

    def second_begin(part):
        nonlocal name
        name = f"again_{part}_{switch_at - 1}"
        kept = [own[n] for n in range(len(first))]
        keep, send = pick_own(second[part], own_perm, kept)
        own2[part], away2[part] = keep, swapped(send, levels[switch_at], f"send_{part}_late")
        if len(arrived) == len(first):
            gather(part)

    def gather(part):
        nonlocal name
        name = f"early_{part}"
        parts = [away[n] for n in range(len(first))]
        early[part] = pick_early(second[part], *other_perm, parts)

    def second_step(part, step):
        nonlocal name, out
        step += switch_at - 1
        name = f"again_{part}_{step}"
        w = factor_terms[step]
        if step == level_count - 1:
            out = last(second[part], w, closing_terms, own2[part], away2[part], out)
            return
        if step == switch_at:
            keep, send = switch(w, own2[part], early[part], away2[part])
        else:
            keep, send = level(w, own2[part], away2[part])
        own2[part], away2[part] = keep, swapped(send, levels[step + 1], f"send_{part}_{step + 1}")

    own2, away2, out = {}, {}, None
    in_turn(
        (FIRST_STARTS, switch_at + 1, first_begin, first_step),
        (SECOND_STARTS, level_count - switch_at, second_begin, second_step),
    )
    return out


def solution(mesh):
    return jax.shard_map(
        per_device,
        mesh=mesh,
        in_specs=(
            P(("grp", "dev"), None, None, None),
            P(("grp", "dev"), None, None),
            P(("grp", "dev"), None, None, None),
            P(None, ("grp", "dev"), None, None, None),
            P(("grp", "dev"), None, None, None),
            P(("grp", "dev"), None),
            P(),
        ),
        out_specs=P(("grp", "dev"), None, None, None),
        check_vma=False,
    )
```
